32 devices in a mesh: rad: 2 (over x), ang: 8 (over z, y), ax: 2 (over core).
Axes of the slice: x: 2, y: 2, z: 4, core: 2. Of those that a mesh axis runs over, the one named last changes fastest.
Arguments:
- start_potential: float32 [32, 384, 256], P('rad', 'ang', 'ax'), may hold values from -6 to 6
- charge_density: float32 [32, 384, 256], P('rad', 'ang', 'ax'), may hold values from -12 to 12
- box_anchor: int32 [3, 128], replicated, may hold values from 0 to 7, as said below
- box_extent: int32 [3, 128], replicated, may hold values from 1 to 2, as said below
- atom_center: float32 [3, 128], replicated, as said below
- atom_charge: float32 [128], replicated, may hold values from 0.5 to 2
- atom_place: int32 [128], replicated, may hold values from 0 to 127, each once
Outputs:
- potential: float32 [32, 384, 256], P('rad', 'ang', 'ax')
- forces: float32 [3, 128], P(None, ('rad', 'ang', 'ax'))
The draws below stay inside these ranges and needn't reach their ends.
Inputs may be any that keep to these rules, and one draw needn't show every extreme that they name: `box_anchor`: box anchors per dimension lie within that dimension's block count, the radial anchor plus extent never passes the last radial block, and at most 8 atoms share one anchor block. `box_extent`: at most 64 atom boxes cover any one block, and in every draw some block is covered by exactly 64. `atom_center`: each atom's center lies inside its box, in the box's unwrapped cell coordinates.
All inputs are finite; a program needn't handle non-finite values.
Results may differ from the reference program's by a relative error of at most 0.0003.
Values sent between devices are 32-bit elements; how exact they have to be, the bound alone decides.
No kernel may reach another device: no remote copies, remote signals or barrier semaphores. Data moves between devices by JAX's collectives and lax.ppermute only.
A program may use at most 64 MiB of HBM per device.

```python
import math
import jax
import jax.numpy as jnp
from jax import lax

CR = 16
CA = 48
CZ = 128
SWEEPS = 3
ATOM_DEV = 4
HOME_MOST = 8
NATOMS = 128
NR = 32
NA = 384
NZ = 256
N_RAD = 2
N_ANG = 8
N_AX = 2


def box_layout(key):
    blocks = N_RAD * N_ANG * N_AX
    slots_all = blocks * HOME_MOST
    folded = jax.random.fold_in(key, 4021)
    key_rank, key_wall, key_spot, key_span, key_order = jax.random.split(folded, 5)
    slot_ids = jnp.arange(slots_all, dtype=jnp.int32)
    home_block = slot_ids // HOME_MOST
    home_r = home_block // (N_ANG * N_AX)
    home_a = home_block // N_AX % N_ANG
    home_z = home_block % N_AX
    wall_flags = jax.random.randint(key_wall, (N_RAD,), 0, 2, dtype=jnp.int32)
    cluster_r = jax.random.randint(jax.random.fold_in(key_spot, 1), (), 1, N_RAD, dtype=jnp.int32)
    cluster_a = jax.random.randint(jax.random.fold_in(key_spot, 2), (), 0, N_ANG, dtype=jnp.int32)
    cluster_z = jax.random.randint(jax.random.fold_in(key_spot, 3), (), 0, N_AX, dtype=jnp.int32)
    back_r = cluster_r - home_r
    back_a = jnp.remainder(cluster_a - home_a, N_ANG)
    back_z = jnp.remainder(cluster_z - home_z, N_AX)
    cluster = (back_r >= 0) & (back_r <= 1) & (back_a <= 1) & (back_z <= 1)
    noise_bits = jax.random.randint(key_rank, (slots_all,), 0, 2 ** 17, dtype=jnp.int32)
    ranking = (noise_bits + wall_flags[home_r] * 2 ** 17 + cluster.astype(jnp.int32) * 2 ** 18) * slots_all + slot_ids
    chosen = lax.top_k(ranking, ATOM_DEV * blocks)[1]
    chosen = chosen[jax.random.permutation(key_order, ATOM_DEV * blocks)]
    anchor = jnp.stack([home_r[chosen], home_a[chosen], home_z[chosen]])
    reach_back = jnp.stack([back_r[chosen], back_a[chosen], back_z[chosen]])
    inside = cluster[chosen]
    extent = jax.random.randint(key_span, (3, ATOM_DEV * blocks), 1, 3, dtype=jnp.int32)
    extent = jnp.where(inside[None, :], jnp.maximum(extent, reach_back + 1), extent)
    outermost = anchor[0] == N_RAD - 1
    extent = extent.at[0].set(jnp.where(outermost, 1, extent[0]))
    return (anchor.astype(jnp.int32), extent.astype(jnp.int32))


def draw_box_anchor(key, part):
    return box_layout(key)[0]


def draw_box_extent(key, part):
    return box_layout(key)[1]


def draw_atom_center(key, part):
    anchor, extent = box_layout(key)
    fraction = jax.random.uniform(jax.random.fold_in(key, 77), anchor.shape, jnp.float32, 0.25, 0.75)
    block_cells = jnp.array([CR, CA, CZ], jnp.float32)[:, None]
    return (anchor.astype(jnp.float32) + fraction * extent.astype(jnp.float32)) * block_cells


def block_levels(stream_key, shape, cuts, least, high):
    gain = 1.0
    for dim, blocks in cuts:
        steps = jax.random.uniform(jax.random.fold_in(jax.random.fold_in(stream_key, 6), dim), (blocks,), jnp.float32, least / len(cuts), high / len(cuts))
        gain = gain * jnp.repeat(jnp.exp(steps), shape[dim] // blocks).reshape((-1,) + (1,) * (len(shape) - 1 - dim))
    return gain


def gaussian(rng, shape, deviation, bound, cuts=(), kind=jnp.bfloat16):
    entries = jax.random.normal(rng, shape, jnp.float32) * deviation
    if len(cuts) > 0:
        entries = block_levels(rng, shape, cuts, -0.22, 0.18) * entries
    return jnp.clip(entries, min=-bound, max=bound).astype(kind)


def setup_inputs(seed: int = 0) -> dict:
    seeds = jax.random.split(jax.random.key(seed), 8)
    start_potential = gaussian(seeds[0], (NR, NA, NZ), 1.0, 6.0, ((0, 2), (1, 8), (2, 2)), jnp.float32)
    charge_density = gaussian(seeds[1], (NR, NA, NZ), 2.0, 12.0, ((0, 2), (1, 8), (2, 2)), jnp.float32)
    box_anchor = draw_box_anchor(jax.random.fold_in(seeds[7], 71), 0)
    box_extent = draw_box_extent(jax.random.fold_in(seeds[7], 71), 0)
    atom_center = draw_atom_center(jax.random.fold_in(seeds[7], 71), 0)
    atom_charge = jnp.clip(jnp.exp(jax.random.uniform(seeds[5], (NATOMS,), jnp.float32, math.log(0.5), math.log(2.0))), 0.5, 2.0)
    atom_place = jax.random.permutation(seeds[6], NATOMS).astype(jnp.int32)
    return dict(start_potential=start_potential, charge_density=charge_density, box_anchor=box_anchor, box_extent=box_extent, atom_center=atom_center, atom_charge=atom_charge, atom_place=atom_place)


cheb_low = 0.2
cheb_high = 2.0
highest = lax.Precision.HIGHEST

def sweep_weights(total_sweeps):
    middle = 0.5 * (cheb_high + cheb_low)
    spread = 0.5 * (cheb_high - cheb_low)
    return [1.0 / (middle + spread * math.cos(math.pi * (2 * number + 1) / (2 * total_sweeps))) for number in range(total_sweeps)]

def relax_step(center, radial_up, radial_down, angle_next, angle_prev, axial_next, axial_prev, source, radius, angle_step, weight):
    lower_face = radius - 0.5
    upper_face = radius + 0.5
    angular = 1.0 / (radius * radius * (angle_step * angle_step))
    doubled = 2.0 * center
    applied = (upper_face * (center - radial_up) + lower_face * (center - radial_down)) / radius
    applied = applied + angular * (doubled - angle_next - angle_prev) + (doubled - axial_next - axial_prev)
    diagonal = (upper_face + lower_face) / radius + 2.0 * angular + 2.0
    return center + weight * (source - applied) / diagonal

def gaussian_pair(coords, middle_point, width):
    distance = coords - middle_point
    profile = jnp.exp(-(distance * distance) / (2.0 * width * width))
    return (profile, profile * (-distance / (width * width)))

def take_plane(potential, plane_index):
    inside = (plane_index >= 0) & (plane_index < NR)
    clamped = jnp.clip(plane_index, 0, NR - 1).astype(jnp.int32)
    layer = lax.dynamic_index_in_dim(potential, clamped, 0, keepdims=False)
    return jnp.where(inside, layer, jnp.zeros_like(layer))

def plane_update(potential, source_field, weight, angle_step, plane_index):
    center = take_plane(potential, plane_index)
    radial_up = take_plane(potential, plane_index + 1)
    radial_down = take_plane(potential, plane_index - 1)
    source = take_plane(source_field, plane_index)
    radius = 0.5 * NR + plane_index.astype(jnp.float32) + 0.5
    return relax_step(center, radial_up, radial_down, jnp.roll(center, -1, 0), jnp.roll(center, 1, 0), jnp.roll(center, -1, 1), jnp.roll(center, 1, 1), source, radius, angle_step, weight)

def atom_force(padded, anchor, extent, center_pos, charge, angle_step):
    width_rad = CR / 3.0
    width_ang = CA / 3.0
    width_axial = CZ / 3.0
    amplitude = 1.0 / math.sqrt(width_ang * width_axial / width_rad)
    zero_start = (anchor[2] * 0).astype(jnp.int32)
    slab = lax.dynamic_slice(padded, ((anchor[0] * CR).astype(jnp.int32), (anchor[1] * CA).astype(jnp.int32), zero_start), (2 * CR, 2 * CA, NZ))
    local_rad = jnp.arange(2 * CR, dtype=jnp.int32)
    coord_rad = (anchor[0] * CR + local_rad).astype(jnp.float32)
    rad_profile, rad_slope = gaussian_pair(coord_rad, center_pos[0], width_rad)
    keep_rad = local_rad < extent[0] * CR
    rad_profile = jnp.where(keep_rad, rad_profile, 0.0)
    rad_slope = jnp.where(keep_rad, rad_slope, 0.0)
    radius = 0.5 * NR + coord_rad + 0.5
    local_ang = jnp.arange(2 * CA, dtype=jnp.int32)
    coord_ang = (anchor[1] * CA + local_ang).astype(jnp.float32)
    ang_profile, ang_slope = gaussian_pair(coord_ang, center_pos[1], width_ang)
    keep_ang = local_ang < extent[1] * CA
    ang_profile = jnp.where(keep_ang, ang_profile, 0.0)
    ang_slope = jnp.where(keep_ang, ang_slope, 0.0)
    cells_axial = jnp.arange(NZ, dtype=jnp.int32)
    shifted = jnp.remainder(cells_axial - anchor[2] * CZ, NZ)
    coord_axial = (anchor[2] * CZ + shifted).astype(jnp.float32)
    axial_profile, axial_slope = gaussian_pair(coord_axial, center_pos[2], width_axial)
    keep_axial = shifted < extent[2] * CZ
    axial_profile = jnp.where(keep_axial, axial_profile, 0.0)
    axial_slope = jnp.where(keep_axial, axial_slope, 0.0)
    factors = jnp.stack([axial_profile, axial_slope], axis=1)
    projected = jnp.dot(slab.reshape(4 * CR * CA, NZ), factors, precision=highest, preferred_element_type=jnp.float32).reshape(2 * CR, 2 * CA, 2)
    along_r = jnp.einsum('ij,j->i', projected[:, :, 0], ang_profile, precision=highest)
    along_a = jnp.einsum('ij,j->i', projected[:, :, 0], ang_slope, precision=highest)
    along_z = jnp.einsum('ij,j->i', projected[:, :, 1], ang_profile, precision=highest)
    weight_rad = angle_step * radius
    force_r = jnp.sum(weight_rad * rad_slope * along_r)
    force_a = jnp.sum(rad_profile * along_a)
    force_z = jnp.sum(weight_rad * rad_profile * along_z)
    return jnp.stack([force_r, force_a, force_z]) * (charge * amplitude)

def reference(start_potential, charge_density, box_anchor, box_extent, atom_center, atom_charge, atom_place):
    angle_step = 2.0 * math.pi / NA
    weights = sweep_weights(SWEEPS)
    potential = start_potential
    planes = jnp.arange(NR, dtype=jnp.int32)
    for sweep_index in range(SWEEPS):
        current = potential
        potential = lax.map(lambda plane_index: plane_update(current, charge_density, weights[sweep_index], angle_step, plane_index), planes)
    padded = jnp.concatenate([potential, potential[:, :CA]], axis=1)
    padded = jnp.concatenate([padded, jnp.zeros((CR, NA + CA, NZ), jnp.float32)], axis=0)

    def one_atom(atom_index):
        return atom_force(padded, box_anchor[:, atom_index], box_extent[:, atom_index], atom_center[:, atom_index], atom_charge[atom_index], angle_step)
    by_atom = lax.map(one_atom, jnp.arange(NATOMS, dtype=jnp.int32))
    forces = jnp.zeros((3, NATOMS), jnp.float32).at[:, atom_place].set(by_atom.T)
    return (potential, forces)
```

```python
import functools
import math

import jax
import jax.numpy as jnp
from jax import lax
from jax.experimental import pallas as pl
from jax.experimental.pallas import tpu as pltpu
from jax.sharding import PartitionSpec as P

SWEEPS = 3
LANES = 128
AXES = ("rad", "ang", "ax")

cheb_low = 0.2
cheb_high = 2.0
highest = lax.Precision.HIGHEST


def sweep_weights(total_sweeps):
    middle = 0.5 * (cheb_high + cheb_low)
    spread = 0.5 * (cheb_high - cheb_low)
    return [
        1.0 / (middle + spread * math.cos(math.pi * (2 * number + 1) / (2 * total_sweeps)))
        for number in range(total_sweeps)
    ]


class Plan:
    def __init__(self, mesh, block, atoms):
        self.n_rad, self.n_ang, self.n_ax = (mesh.shape[name] for name in AXES)
        self.cells_r, self.cells_a, self.cells_z = block
        self.atoms = atoms
        self.chunks = atoms // LANES
        self.ring = self.cells_a + 8
        self.total_r = self.cells_r * self.n_rad
        self.total_a = self.cells_a * self.n_ang
        self.total_z = self.cells_z * self.n_ax
        self.angle_step = 2.0 * math.pi / self.total_a
        self.sides = 0 if self.n_rad == 1 else 1 if self.n_rad == 2 else 2
        self.slots = self.cells_r + SWEEPS * self.sides
        self.guard = SWEEPS + 1

    def sign(self, side, rad):
        if self.sides == 1:
            return 1 - 2 * rad
        return 1 - 2 * side

    def side_row(self, side, rad, step):
        sign = self.sign(side, rad)
        return (self.cells_r - 1) * (1 + sign) // 2 + sign * step

    def landing_row(self, side, rad, step):
        sign = self.sign(side, rad)
        return (self.cells_r - 1) * (1 + sign) // 2 - sign * (step - 1)

    def device(self, rad, ang, ax):
        return (rad * self.n_ang + ang) * self.n_ax + ax

    def pairs(self, core, move):
        found = []
        for rad in range(self.n_rad):
            for ang in range(self.n_ang):
                target = move(rad, ang)
                if target is not None:
                    found.append((self.device(rad, ang, core), self.device(*target, core)))
        return found


def factors_kernel(plan, anchor, extent, center, charge, place, z_out, a_out, r_out):
    rad, ang, ax = (lax.axis_index(name) for name in AXES)
    width_r, width_a, width_z = plan.cells_r / 3.0, plan.cells_a / 3.0, plan.cells_z / 3.0
    amplitude = 1.0 / math.sqrt(width_a * width_z / width_r)
    table = jnp.concatenate(
        [
            anchor[...].astype(jnp.float32),
            extent[...].astype(jnp.float32),
            center[...],
            charge[...],
            jnp.zeros((6, plan.atoms), jnp.float32),
        ],
        axis=0,
    )

    def pair(cell, start, span, middle, width, total):
        shifted = cell - start
        if total is not None:
            shifted = jnp.where(shifted < 0.0, shifted + total, shifted)
        distance = shifted + start - middle
        inside = (shifted >= 0.0) & (shifted < span)
        profile = jnp.where(inside, jnp.exp(-(distance * distance) / (2.0 * width * width)), 0.0)
        return profile, profile * (-distance / (width * width))

    def chunk(number, carry):
        rows = lax.broadcasted_iota(jnp.int32, (LANES, plan.atoms), 0) + number * LANES
        onehot = (place[...] == rows).astype(jnp.float32)
        ordered = lax.dot_general(
            table,
            onehot,
            (((1,), (1,)), ((), ())),
            precision=highest,
            preferred_element_type=jnp.float32,
        )
        row = [ordered[k : k + 1, :] for k in range(10)]
        depth = lax.broadcasted_iota(jnp.int32, (plan.total_z, LANES), 0) + ax * plan.cells_z
        depth = jnp.where(depth >= plan.total_z, depth - plan.total_z, depth).astype(jnp.float32)
        profile, slope = pair(
            depth, row[2] * plan.cells_z, row[5] * plan.cells_z, row[8], width_z, plan.total_z
        )
        z_out[number, :, :LANES] = profile
        z_out[number, :, LANES:] = slope
        spot = lax.broadcasted_iota(jnp.int32, (plan.ring, LANES), 0)
        spot = jnp.where(spot < plan.cells_a + 4, spot, spot - plan.ring) + ang * plan.cells_a
        spot = jnp.where(spot < 0, spot + plan.total_a, spot)
        spot = jnp.where(spot >= plan.total_a, spot - plan.total_a, spot).astype(jnp.float32)
        profile, slope = pair(
            spot, row[1] * plan.cells_a, row[4] * plan.cells_a, row[7], width_a, plan.total_a
        )
        a_out[number, 0] = profile
        a_out[number, 1] = slope
        slot = lax.broadcasted_iota(jnp.int32, (plan.slots, LANES), 0)
        level = slot
        for side in range(plan.sides):
            first = plan.cells_r + SWEEPS * side
            level = jnp.where(slot >= first, plan.side_row(side, rad, slot - first + 1), level)
        level = (level + rad * plan.cells_r).astype(jnp.float32)
        profile, slope = pair(
            level, row[0] * plan.cells_r, row[3] * plan.cells_r, row[6], width_r, None
        )
        radius = 0.5 * plan.total_r + level + 0.5
        strength = row[9] * amplitude
        r_out[number, 0] = strength * (plan.angle_step * radius) * slope
        r_out[number, 1] = strength * profile
        r_out[number, 2] = strength * (plan.angle_step * radius) * profile
        return carry

    if plan.chunks == 1:
        chunk(0, 0)
    else:
        lax.fori_loop(0, plan.chunks, chunk, 0)


def sweeps_kernel(
    plan,
    pot_own,
    pot_other,
    rho_own,
    rho_other,
    z_fac,
    a_fac,
    r_fac,
    own_out,
    hal_out,
    rad_out,
    force_out,
    first,
    second,
    grown,
    coef,
):
    rad, ax = lax.axis_index("rad"), lax.axis_index("ax")
    guard, rows, ring, depth = plan.guard, plan.cells_r, plan.ring, plan.total_z
    weights = sweep_weights(SWEEPS)

    level = lax.broadcasted_iota(jnp.int32, (coef.shape[1], depth), 0) - guard + rad * rows
    valid = (level >= 0) & (level < plan.total_r)
    radius = 0.5 * plan.total_r + level.astype(jnp.float32) + 0.5
    upper, lower = (radius + 0.5) / radius, (radius - 0.5) / radius
    angular = 1.0 / (radius * radius * (plan.angle_step * plan.angle_step))
    diagonal = upper + lower + 2.0 * angular + 2.0
    inverse = jnp.where(valid, 1.0 / diagonal, 0.0)
    coef[0] = upper
    coef[1] = lower
    coef[2] = angular
    coef[3] = inverse

    blank = jnp.zeros((ring, depth), jnp.float32)
    for buffer in (first, second):
        for row in range(guard):
            buffer[row] = blank
            buffer[guard + rows + row] = blank
    tail = jnp.zeros((ring - plan.cells_a, depth), jnp.float32)

    def whole(own, other, row):
        return jnp.concatenate([jnp.concatenate([own[row], other[row]], axis=1), tail], axis=0)

    for row in range(rows):
        first[guard + row] = whole(pot_own, pot_other, row)

    def relaxed(source, row, weight, charge):
        center = source[row]
        up, down, turn, inverse = (coef[k, pl.ds(row, 1), :] for k in range(4))
        total = pltpu.roll(center, 1, 1) + pltpu.roll(center, depth - 1, 1)
        total += turn * (pltpu.roll(center, 1, 0) + pltpu.roll(center, ring - 1, 0))
        total += up * source[row + 1] + down * source[row - 1]
        if charge is not None:
            total += charge
        return (1.0 - weight) * center + (weight * inverse) * total

    source, target = first, second
    for sweep in range(SWEEPS):
        last = sweep == SWEEPS - 1
        for row in range(rows):
            fresh = relaxed(source, guard + row, weights[sweep], whole(rho_own, rho_other, row))
            if last:
                grown[row] = fresh
                own_out[row] = fresh[: plan.cells_a, : plan.cells_z]
                hal_out[row] = fresh[plan.cells_a :, :]
            else:
                target[guard + row] = fresh
        for side in range(plan.sides):
            for step in range(1, sweep + 2):
                place = guard + plan.side_row(side, rad, step)
                fresh = relaxed(source, place, weights[sweep], None)
                if last:
                    slot = SWEEPS * side + step - 1
                    grown[rows + slot] = fresh
                    rad_out[slot] = fresh
                else:
                    target[place] = fresh
        source, target = target, source

    force_out[...] = jnp.zeros_like(force_out)

    @pl.when(ax == plan.n_ax - 1)
    def _():
        def chunk(number, carry):
            spread = jnp.dot(
                grown[...].reshape(plan.slots * ring, depth),
                z_fac[number],
                precision=highest,
                preferred_element_type=jnp.float32,
            )
            sums = [jnp.zeros((ring, LANES), jnp.float32) for _ in range(3)]
            for slot in range(plan.slots):
                piece = spread[slot * ring : (slot + 1) * ring]
                for k, part in enumerate((piece[:, :LANES], piece[:, :LANES], piece[:, LANES:])):
                    sums[k] += r_fac[number, k, pl.ds(slot, 1), :] * part
            for k, turn in enumerate((0, 1, 0)):
                force_out[number, pl.ds(k, 1), :] = jnp.sum(
                    a_fac[number, turn] * sums[k], axis=0, keepdims=True
                )
            return carry

        if plan.chunks == 1:
            chunk(0, 0)
        else:
            lax.fori_loop(0, plan.chunks, chunk, 0)


def turn_kernel(plan, *refs):
    hal, landed = refs[0], refs[1 : 1 + plan.sides]
    even_out, odd_out, held = refs[1 + plan.sides :]
    rad, ang = lax.axis_index("rad"), lax.axis_index("ang")
    held[...] = hal[...]
    for side in range(plan.sides):
        for step in range(1, SWEEPS + 1):
            row = plan.landing_row(side, rad, step)
            held[row] = held[row] + landed[side][step - 1, plan.cells_a :, :]
    low_half = lax.broadcasted_iota(jnp.int32, (8, plan.total_z), 0) < 4
    is_even = (lax.broadcasted_iota(jnp.int32, (8, plan.total_z), 0) * 0 + ang) % 2 == 0
    for tile in range(plan.cells_r // 2):
        front, back = held[2 * tile], held[2 * tile + 1]
        above = jnp.where(low_half, front, pltpu.roll(back, 4, 0))
        below = jnp.where(low_half, pltpu.roll(front, 4, 0), back)
        even_out[tile] = jnp.where(is_even, above, below)
        odd_out[tile] = jnp.where(is_even, below, above)


def final_kernel(plan, *refs):
    own, here, there, out = refs[0], refs[1 : 3 + plan.sides], refs[3 + plan.sides : -1], refs[-1]
    rad, ang = lax.axis_index("rad"), lax.axis_index("ang")
    width = plan.cells_z

    def landed(number, index):
        return here[number][index][:, :width] + there[number][index][:, width:]

    low_half = lax.broadcasted_iota(jnp.int32, (8, width), 0) < 4
    is_even = (lax.broadcasted_iota(jnp.int32, (8, width), 0) * 0 + ang) % 2 == 0
    top = plan.cells_a - 8
    for tile in range(plan.cells_r // 2):
        even, odd = landed(plan.sides, tile), landed(plan.sides + 1, tile)
        above, below = jnp.where(is_even, even, odd), jnp.where(is_even, odd, even)
        for half in range(2):
            row = 2 * tile + half
            from_below = below if half == 0 else pltpu.roll(below, 4, 0)
            from_above = above if half == 1 else pltpu.roll(above, 4, 0)
            out[row] = own[row]
            out[row, 0:8, :] += jnp.where(low_half, from_below, 0.0)
            out[row, top:, :] += jnp.where(low_half, 0.0, from_above)
    for side in range(plan.sides):
        for step in range(1, SWEEPS + 1):
            row = plan.landing_row(side, rad, step)
            out[row] += landed(side, step - 1)[: plan.cells_a]


def call(kernel, plan, outs, scratch, flops, bytes_moved, args):
    in_vmem = pl.BlockSpec(memory_space=pltpu.VMEM)
    return pl.pallas_call(
        functools.partial(kernel, plan),
        out_shape=[jax.ShapeDtypeStruct(shape, jnp.float32) for shape in outs],
        in_specs=[in_vmem] * len(args),
        out_specs=[in_vmem] * len(outs),
        scratch_shapes=[pltpu.VMEM(shape, jnp.float32) for shape in scratch],
        compiler_params=pltpu.CompilerParams(vmem_limit_bytes=24 * 2**20),
        cost_estimate=pl.CostEstimate(flops=flops, bytes_accessed=bytes_moved, transcendentals=0),
    )(*args)


def shards(plan, potential, density, anchor, extent, center, charge, place):
    ring, depth, slots, chunks = plan.ring, plan.total_z, plan.slots, plan.chunks
    rows = plan.cells_r
    swap = [(0, 1), (1, 0)]
    potential_other = lax.ppermute(potential, "ax", swap)
    density_other = lax.ppermute(density, "ax", swap)
    factors = call(
        factors_kernel,
        plan,
        [(chunks, depth, 2 * LANES), (chunks, 2, ring, LANES), (chunks, 3, slots, LANES)],
        [],
        10**6,
        10**6,
        (anchor, extent, center, charge.reshape(1, -1), place.reshape(1, -1)),
    )
    outs = [(rows, plan.cells_a, plan.cells_z), (rows, 8, depth)]
    outs += [(max(1, SWEEPS * plan.sides), ring, depth), (chunks, 8, LANES)]
    tall = rows + 2 * plan.guard
    scratch = [(tall, ring, depth)] * 2 + [(slots, ring, depth), (4, tall, depth)]
    own, hal, side_rows, force = call(
        sweeps_kernel,
        plan,
        outs,
        scratch,
        10**9,
        10**7,
        (potential, potential_other, density, density_other, *factors),
    )

    core, messenger = 0, plan.n_ax - 1

    def send(value, perm):
        return lax.ppermute(value, AXES, perm)

    landed = []
    if plan.sides == 1:
        landed.append(send(side_rows, plan.pairs(core, lambda r, a: (1 - r, a))))
    elif plan.sides == 2:
        down = plan.pairs(core, lambda r, a: (r - 1, a) if r > 0 else None)
        up = plan.pairs(core, lambda r, a: (r + 1, a) if r + 1 < plan.n_rad else None)
        landed.append(send(side_rows[SWEEPS:], down))
        landed.append(send(side_rows[:SWEEPS], up))
    packed = (rows // 2, 8, depth)
    even, odd = call(
        turn_kernel, plan, [packed] * 2, [(rows, 8, depth)], 10**5, 10**6, (hal, *landed)
    )
    landed.append(send(even, plan.pairs(core, lambda r, a: (r, a ^ 1))))
    landed.append(send(odd, plan.pairs(core, lambda r, a: (r, (a + 1 - 2 * (1 - a % 2)) % plan.n_ang))))

    for axis, count in ((0, plan.n_rad), (1, plan.n_ang)):
        step = 1
        while step < count:
            moved = lambda r, a, step=step: (r ^ step, a) if axis == 0 else (r, a ^ step)
            force = force + send(force, plan.pairs(messenger, moved))
            step *= 2

    hand_on = [(0, messenger)]
    handed = [lax.ppermute(value, "ax", hand_on) for value in landed]
    force = force + lax.ppermute(force, "ax", [(messenger, 0)])
    (final,) = call(
        final_kernel,
        plan,
        [(rows, plan.cells_a, plan.cells_z)],
        [],
        10**5,
        10**6,
        (own, *landed, *handed),
    )
    devices = plan.n_rad * plan.n_ang * plan.n_ax
    share = plan.atoms // devices
    rank = plan.device(*(lax.axis_index(name) for name in AXES))
    first = rank * share
    mine = lax.dynamic_slice(force, (first // LANES, 0, first % LANES), (1, 3, share))
    return final, mine.reshape(3, share)


def solution(mesh):
    whole = P("rad", "ang", "ax")

    def run(potential, density, anchor, extent, center, charge, place):
        sizes = [mesh.shape[name] for name in AXES]
        block = [total // parts for total, parts in zip(potential.shape, sizes)]
        plan = Plan(mesh, block, charge.shape[0])
        return jax.shard_map(
            functools.partial(shards, plan),
            mesh=mesh,
            in_specs=(whole, whole, P(), P(), P(), P(), P()),
            out_specs=(whole, P(None, AXES)),
            check_vma=False,
        )(potential, density, anchor, extent, center, charge, place)

    return run
```

```python
import functools
import math

import jax
import jax.numpy as jnp
from jax import lax
from jax.experimental import pallas as pl
from jax.experimental.pallas import tpu as pltpu
from jax.sharding import PartitionSpec as P

SWEEPS = 3
LANES = 128
AXES = ("rad", "ang", "ax")

cheb_low = 0.2
cheb_high = 2.0
highest = lax.Precision.HIGHEST


def sweep_weights(total_sweeps):
    middle = 0.5 * (cheb_high + cheb_low)
    spread = 0.5 * (cheb_high - cheb_low)
    return [
        1.0 / (middle + spread * math.cos(math.pi * (2 * number + 1) / (2 * total_sweeps)))
        for number in range(total_sweeps)
    ]


class Plan:
    def __init__(self, mesh, block, atoms):
        self.n_rad, self.n_ang, self.n_ax = (mesh.shape[name] for name in AXES)
        self.cells_r, self.cells_a, self.cells_z = block
        self.atoms = atoms
        self.chunks = atoms // LANES
        self.ring = self.cells_a + 8
        self.total_r = self.cells_r * self.n_rad
        self.total_a = self.cells_a * self.n_ang
        self.total_z = self.cells_z * self.n_ax
        self.angle_step = 2.0 * math.pi / self.total_a
        self.sides = 0 if self.n_rad == 1 else 1 if self.n_rad == 2 else 2
        self.slots = self.cells_r + SWEEPS * self.sides
        self.guard = SWEEPS + 1
        self.side_tiles = self.sides * SWEEPS * (self.ring // 8)

    def sign(self, side, rad):
        if self.sides == 1:
            return 1 - 2 * rad
        return 1 - 2 * side

    def side_row(self, side, rad, step):
        sign = self.sign(side, rad)
        return (self.cells_r - 1) * (1 + sign) // 2 + sign * step

    def landing_row(self, side, rad, step):
        sign = self.sign(side, rad)
        return (self.cells_r - 1) * (1 + sign) // 2 - sign * (step - 1)

    def device(self, rad, ang, ax):
        return (rad * self.n_ang + ang) * self.n_ax + ax

    def moves(self, move):
        found = []
        for rad in range(self.n_rad):
            for ang in range(self.n_ang):
                target = move(rad, ang)
                if target is not None:
                    for ax in range(self.n_ax):
                        found.append((self.device(rad, ang, ax), self.device(*target, 1 - ax)))
        return found


def factors_kernel(plan, *refs):
    sources, (z_out, a_out, r_out, pot_out, rho_out), held = refs[:7], refs[7:12], refs[12:17]
    copies = [
        pltpu.make_async_copy(source, target, refs[17].at[k])
        for k, (source, target) in enumerate(zip(sources, (*held, pot_out, rho_out)))
    ]
    for copy in copies:
        copy.start()
    for copy in copies[:5]:
        copy.wait()
    anchor, extent, center, charge, place = held
    rad, ang, ax = (lax.axis_index(name) for name in AXES)
    width_r, width_a, width_z = plan.cells_r / 3.0, plan.cells_a / 3.0, plan.cells_z / 3.0
    amplitude = 1.0 / math.sqrt(width_a * width_z / width_r)
    table = jnp.concatenate(
        [
            anchor[...].astype(jnp.float32),
            extent[...].astype(jnp.float32),
            center[...],
            charge[...],
            jnp.zeros((6, plan.atoms), jnp.float32),
        ],
        axis=0,
    )

    def pair(cell, start, span, middle, width, total):
        shifted = cell - start
        if total is not None:
            shifted = jnp.where(shifted < 0.0, shifted + total, shifted)
        distance = shifted + start - middle
        inside = (shifted >= 0.0) & (shifted < span)
        profile = jnp.where(inside, jnp.exp(-(distance * distance) / (2.0 * width * width)), 0.0)
        return profile, profile * (-distance / (width * width))

    def chunk(number, carry):
        rows = lax.broadcasted_iota(jnp.int32, (LANES, plan.atoms), 0) + number * LANES
        onehot = (place[...] == rows).astype(jnp.float32)
        ordered = lax.dot_general(
            table,
            onehot,
            (((1,), (1,)), ((), ())),
            precision=highest,
            preferred_element_type=jnp.float32,
        )
        row = [ordered[k : k + 1, :] for k in range(10)]
        depth = lax.broadcasted_iota(jnp.int32, (plan.total_z, LANES), 0) + ax * plan.cells_z
        depth = jnp.where(depth >= plan.total_z, depth - plan.total_z, depth).astype(jnp.float32)
        profile, slope = pair(
            depth, row[2] * plan.cells_z, row[5] * plan.cells_z, row[8], width_z, plan.total_z
        )
        z_out[number, :, :LANES] = profile
        z_out[number, :, LANES:] = slope
        spot = lax.broadcasted_iota(jnp.int32, (plan.ring, LANES), 0)
        spot = jnp.where(spot < plan.cells_a + 4, spot, spot - plan.ring) + ang * plan.cells_a
        spot = jnp.where(spot < 0, spot + plan.total_a, spot)
        spot = jnp.where(spot >= plan.total_a, spot - plan.total_a, spot).astype(jnp.float32)
        profile, slope = pair(
            spot, row[1] * plan.cells_a, row[4] * plan.cells_a, row[7], width_a, plan.total_a
        )
        a_out[number, 0] = profile
        a_out[number, 1] = slope
        slot = lax.broadcasted_iota(jnp.int32, (plan.slots, LANES), 0)
        level = slot
        for side in range(plan.sides):
            first = plan.cells_r + SWEEPS * side
            level = jnp.where(slot >= first, plan.side_row(side, rad, slot - first + 1), level)
        level = (level + rad * plan.cells_r).astype(jnp.float32)
        profile, slope = pair(
            level, row[0] * plan.cells_r, row[3] * plan.cells_r, row[6], width_r, None
        )
        radius = 0.5 * plan.total_r + level + 0.5
        strength = row[9] * amplitude
        r_out[number, 0] = strength * (plan.angle_step * radius) * slope
        r_out[number, 1] = strength * profile
        r_out[number, 2] = strength * (plan.angle_step * radius) * profile
        return carry

    if plan.chunks == 1:
        chunk(0, 0)
    else:
        lax.fori_loop(0, plan.chunks, chunk, 0)
    for copy in copies[5:]:
        copy.wait()


def sweeps_kernel(
    plan,
    pot_own,
    pot_other,
    rho_own,
    rho_other,
    z_fac,
    a_fac,
    r_fac,
    own_out,
    hal_out,
    rad_out,
    first,
    second,
    grown,
    coef,
):
    rad = lax.axis_index("rad")
    guard, rows, ring, depth = plan.guard, plan.cells_r, plan.ring, plan.total_z
    weights = sweep_weights(SWEEPS)

    level = lax.broadcasted_iota(jnp.int32, (coef.shape[1], depth), 0) - guard + rad * rows
    valid = (level >= 0) & (level < plan.total_r)
    radius = 0.5 * plan.total_r + level.astype(jnp.float32) + 0.5
    upper, lower = (radius + 0.5) / radius, (radius - 0.5) / radius
    angular = 1.0 / (radius * radius * (plan.angle_step * plan.angle_step))
    diagonal = upper + lower + 2.0 * angular + 2.0
    inverse = jnp.where(valid, 1.0 / diagonal, 0.0)
    coef[0] = upper
    coef[1] = lower
    coef[2] = angular
    coef[3] = inverse

    blank = jnp.zeros((ring, depth), jnp.float32)
    for buffer in (first, second):
        for row in range(guard):
            buffer[row] = blank
            buffer[guard + rows + row] = blank
    tail = jnp.zeros((ring - plan.cells_a, depth), jnp.float32)

    def whole(own, other, row):
        return jnp.concatenate([jnp.concatenate([own[row], other[row]], axis=1), tail], axis=0)

    for row in range(rows):
        first[guard + row] = whole(pot_own, pot_other, row)

    def relaxed(source, row, weight, charge):
        center = source[row]
        up, down, turn, inverse = (coef[k, pl.ds(row, 1), :] for k in range(4))
        total = pltpu.roll(center, 1, 1) + pltpu.roll(center, depth - 1, 1)
        total += turn * (pltpu.roll(center, 1, 0) + pltpu.roll(center, ring - 1, 0))
        total += up * source[row + 1] + down * source[row - 1]
        if charge is not None:
            total += charge
        return (1.0 - weight) * center + (weight * inverse) * total

    def send_row(slot, fresh):
        tiles = ring // 8
        for tile in range(tiles - 1):
            rad_out[slot * tiles + tile] = fresh[8 * tile : 8 * tile + 8, plan.cells_z :]
        rad_out[slot * tiles + tiles - 1] = fresh[plan.cells_a :, : plan.cells_z]

    source, target = first, second
    for sweep in range(SWEEPS):
        last = sweep == SWEEPS - 1
        for row in range(rows):
            fresh = relaxed(source, guard + row, weights[sweep], whole(rho_own, rho_other, row))
            if last:
                grown[row] = fresh
                own_out[row] = fresh[: plan.cells_a, : plan.cells_z]
                hal_out[row] = fresh[plan.cells_a :, plan.cells_z :]
            else:
                target[guard + row] = fresh
        for side in range(plan.sides):
            for step in range(1, sweep + 2):
                place = guard + plan.side_row(side, rad, step)
                fresh = relaxed(source, place, weights[sweep], None)
                if last:
                    slot = SWEEPS * side + step - 1
                    grown[rows + slot] = fresh
                    send_row(slot, fresh)
                else:
                    target[place] = fresh
        source, target = target, source

    force_base = plan.side_tiles

    def chunk(number, carry):
        spread = jnp.dot(
            grown[...].reshape(plan.slots * ring, depth),
            z_fac[number],
            precision=highest,
            preferred_element_type=jnp.float32,
        )
        sums = [jnp.zeros((ring, LANES), jnp.float32) for _ in range(3)]
        for slot in range(plan.slots):
            piece = spread[slot * ring : (slot + 1) * ring]
            for k, part in enumerate((piece[:, :LANES], piece[:, :LANES], piece[:, LANES:])):
                sums[k] += r_fac[number, k, pl.ds(slot, 1), :] * part
        total = [
            jnp.sum(a_fac[number, turn] * sums[k], axis=0, keepdims=True)
            for k, turn in enumerate((0, 1, 0))
        ]
        total.append(jnp.zeros((5, LANES), jnp.float32))
        rad_out[force_base + number] = jnp.concatenate(total, axis=0)
        return carry

    if plan.chunks == 1:
        chunk(0, 0)
    else:
        lax.fori_loop(0, plan.chunks, chunk, 0)


def turn_kernel(plan, *refs):
    hal, landed, forces = refs[0], refs[1 : 1 + plan.sides], refs[1 + plan.sides : -3]
    even_out, odd_out, held = refs[-3:]
    rad, ang = lax.axis_index("rad"), lax.axis_index("ang")
    width = plan.cells_z
    held[...] = hal[...]
    tiles = plan.ring // 8
    for side in range(plan.sides):
        for step in range(1, SWEEPS + 1):
            row = plan.landing_row(side, rad, step)
            held[row] = held[row] + landed[side][step * tiles - 1]
    low_half = lax.broadcasted_iota(jnp.int32, (8, width), 0) < 4
    is_even = (lax.broadcasted_iota(jnp.int32, (8, width), 0) * 0 + ang) % 2 == 0
    pairs = plan.cells_r // 2
    for tile in range(pairs):
        front, back = held[2 * tile], held[2 * tile + 1]
        above = jnp.where(low_half, front, pltpu.roll(back, 4, 0))
        below = jnp.where(low_half, pltpu.roll(front, 4, 0), back)
        even_out[tile] = jnp.where(is_even, above, below)
        odd_out[tile] = jnp.where(is_even, below, above)
    for number in range(plan.chunks):
        total = forces[0][number - plan.chunks + forces[0].shape[0]]
        if len(forces) > 1:
            total = total + forces[1][number - plan.chunks + forces[1].shape[0]]
        even_out[pairs + number] = total


def final_kernel(plan, *refs):
    own, landed, even_in, odd_in, out = refs[0], refs[1 : 1 + plan.sides], *refs[-3:]
    rad, ang = lax.axis_index("rad"), lax.axis_index("ang")
    width = plan.cells_z
    low_half = lax.broadcasted_iota(jnp.int32, (8, width), 0) < 4
    is_even = (lax.broadcasted_iota(jnp.int32, (8, width), 0) * 0 + ang) % 2 == 0
    top = plan.cells_a - 8
    tiles = plan.ring // 8
    for tile in range(plan.cells_r // 2):
        even, odd = even_in[tile], odd_in[tile]
        above, below = jnp.where(is_even, even, odd), jnp.where(is_even, odd, even)
        for half in range(2):
            row = 2 * tile + half
            from_below = below if half == 0 else pltpu.roll(below, 4, 0)
            from_above = above if half == 1 else pltpu.roll(above, 4, 0)
            out[row] = own[row]
            out[row, 0:8, :] += jnp.where(low_half, from_below, 0.0)
            out[row, top:, :] += jnp.where(low_half, 0.0, from_above)
    for side in range(plan.sides):
        for step in range(1, SWEEPS + 1):
            row = plan.landing_row(side, rad, step)
            for tile in range(tiles - 1):
                out[row, 8 * tile : 8 * tile + 8, :] += landed[side][(step - 1) * tiles + tile]


def call(kernel, plan, outs, scratch, flops, bytes_moved, args, spaces=None):
    in_vmem = pl.BlockSpec(memory_space=pltpu.VMEM)
    return pl.pallas_call(
        functools.partial(kernel, plan),
        out_shape=[jax.ShapeDtypeStruct(shape, jnp.float32) for shape in outs],
        in_specs=spaces or [in_vmem] * len(args),
        out_specs=[in_vmem] * len(outs),
        scratch_shapes=scratch,
        compiler_params=pltpu.CompilerParams(vmem_limit_bytes=24 * 2**20),
        cost_estimate=pl.CostEstimate(flops=flops, bytes_accessed=bytes_moved, transcendentals=0),
    )(*args)


def shards(plan, potential, density, anchor, extent, center, charge, place):
    ring, depth, slots, chunks = plan.ring, plan.total_z, plan.slots, plan.chunks
    rows, width, block = plan.cells_r, plan.cells_z, potential.shape
    swap = [(0, 1), (1, 0)]
    potential_other = lax.ppermute(potential, "ax", swap)
    density_other = lax.ppermute(density, "ax", swap)
    tables = (anchor, extent, center, charge.reshape(1, -1), place.reshape(1, -1))
    *factors, potential, density = call(
        factors_kernel,
        plan,
        [(chunks, depth, 2 * LANES), (chunks, 2, ring, LANES), (chunks, 3, slots, LANES)] + [block] * 2,
        [pltpu.VMEM(table.shape, table.dtype) for table in tables] + [pltpu.SemaphoreType.DMA((7,))],
        10**6,
        10**6,
        (*tables, potential, density),
        [pl.BlockSpec(memory_space=pl.ANY)] * 7,
    )
    tall = rows + 2 * plan.guard
    scratch = [(tall, ring, depth)] * 2 + [(slots, ring, depth), (4, tall, depth)]
    own, hal, sides = call(
        sweeps_kernel,
        plan,
        [block, (rows, 8, width), (plan.side_tiles + chunks, 8, LANES)],
        [pltpu.VMEM(shape, jnp.float32) for shape in scratch],
        10**9,
        10**7,
        (potential, potential_other, density, density_other, *factors),
    )

    def send(value, move):
        return lax.ppermute(value, AXES, plan.moves(move))

    per_side = plan.side_tiles // max(1, plan.sides)
    if plan.sides == 1:
        landed = [send(sides, lambda r, a: (1 - r, a))]
        forces = [sides, landed[0]]
    else:
        landed = []
        force = sides[plan.side_tiles :]
        if plan.sides == 2:
            landed.append(send(sides[per_side : 2 * per_side], lambda r, a: (r - 1, a) if r else None))
            last = plan.n_rad - 1
            landed.append(send(sides[:per_side], lambda r, a: (r + 1, a) if r < last else None))
        step = 1
        while step < plan.n_rad:
            force = force + send(force, lambda r, a: (r ^ step, a))
            step *= 2
        forces = [force]
    pairs = rows // 2
    even, odd = call(
        turn_kernel,
        plan,
        [(pairs + chunks, 8, width), (pairs, 8, width)],
        [pltpu.VMEM((rows, 8, width), jnp.float32)],
        10**5,
        10**6,
        (hal, *landed, *forces),
    )
    odd_in = send(odd, lambda r, a: (r, (a + 1 - 2 * (1 - a % 2)) % plan.n_ang))
    even_in = send(even, lambda r, a: (r, a ^ 1))
    force = even[pairs:] + even_in[pairs:]
    step = 2
    while step < plan.n_ang:
        force = force + send(force, lambda r, a: (r, a ^ step))
        step *= 2
    (final,) = call(
        final_kernel, plan, [block], [], 10**5, 10**6, (own, *landed, even_in, odd_in)
    )
    share = plan.atoms // (plan.n_rad * plan.n_ang * plan.n_ax)
    first = plan.device(*(lax.axis_index(name) for name in AXES)) * share
    mine = lax.dynamic_slice(force, (first // LANES, 0, first % LANES), (1, 3, share))
    return final, mine.reshape(3, share)


def solution(mesh):
    whole = P("rad", "ang", "ax")

    def run(potential, density, anchor, extent, center, charge, place):
        sizes = [mesh.shape[name] for name in AXES]
        block = [total // parts for total, parts in zip(potential.shape, sizes)]
        plan = Plan(mesh, block, charge.shape[0])
        return jax.shard_map(
            functools.partial(shards, plan),
            mesh=mesh,
            in_specs=(whole, whole, P(), P(), P(), P(), P()),
            out_specs=(whole, P(None, AXES)),
            check_vma=False,
        )(potential, density, anchor, extent, center, charge, place)

    return run
```

```python
import functools
import math

import jax
import jax.numpy as jnp
from jax import lax
from jax.experimental import pallas as pl
from jax.experimental.pallas import tpu as pltpu
from jax.sharding import PartitionSpec as P

SWEEPS = 3
LANES = 128
AXES = ("rad", "ang", "ax")

cheb_low = 0.2
cheb_high = 2.0
highest = lax.Precision.HIGHEST


def sweep_weights(total_sweeps):
    middle = 0.5 * (cheb_high + cheb_low)
    spread = 0.5 * (cheb_high - cheb_low)
    return [
        1.0 / (middle + spread * math.cos(math.pi * (2 * number + 1) / (2 * total_sweeps)))
        for number in range(total_sweeps)
    ]


class Plan:
    def __init__(self, mesh, block, atoms):
        self.n_rad, self.n_ang, self.n_ax = (mesh.shape[name] for name in AXES)
        self.cells_r, self.cells_a, self.cells_z = block
        self.atoms = atoms
        self.chunks = atoms // LANES
        self.ring = self.cells_a + 8
        self.total_r = self.cells_r * self.n_rad
        self.total_a = self.cells_a * self.n_ang
        self.total_z = self.cells_z * self.n_ax
        self.angle_step = 2.0 * math.pi / self.total_a
        self.sides = 0 if self.n_rad == 1 else 1 if self.n_rad == 2 else 2
        self.slots = self.cells_r + SWEEPS * self.sides
        self.guard = SWEEPS + 1
        self.side_tiles = self.sides * SWEEPS * (self.ring // 8)

    def sign(self, side, rad):
        if self.sides == 1:
            return 1 - 2 * rad
        return 1 - 2 * side

    def side_row(self, side, rad, step):
        sign = self.sign(side, rad)
        return (self.cells_r - 1) * (1 + sign) // 2 + sign * step

    def landing_row(self, side, rad, step):
        sign = self.sign(side, rad)
        return (self.cells_r - 1) * (1 + sign) // 2 - sign * (step - 1)

    def device(self, rad, ang, ax):
        return (rad * self.n_ang + ang) * self.n_ax + ax

    def moves(self, move):
        found = []
        for rad in range(self.n_rad):
            for ang in range(self.n_ang):
                target = move(rad, ang)
                if target is not None:
                    for ax in range(self.n_ax):
                        found.append((self.device(rad, ang, ax), self.device(*target, 1 - ax)))
        return found


def factors_kernel(plan, *refs):
    sources, (z_out, a_out, r_out, pot_out, rho_out), held = refs[:7], refs[7:12], refs[12:17]
    copies = [
        pltpu.make_async_copy(source, target, refs[17].at[k])
        for k, (source, target) in enumerate(zip(sources, (*held, pot_out, rho_out)))
    ]
    for copy in copies:
        copy.start()
    for copy in copies[:5]:
        copy.wait()
    anchor, extent, center, charge, place = held
    rad, ang, ax = (lax.axis_index(name) for name in AXES)
    width_r, width_a, width_z = plan.cells_r / 3.0, plan.cells_a / 3.0, plan.cells_z / 3.0
    amplitude = 1.0 / math.sqrt(width_a * width_z / width_r)
    table = jnp.concatenate(
        [
            anchor[...].astype(jnp.float32),
            extent[...].astype(jnp.float32),
            center[...],
            charge[...],
            jnp.zeros((6, plan.atoms), jnp.float32),
        ],
        axis=0,
    )

    def pair(cell, start, span, middle, width, total):
        shifted = cell - start
        if total is not None:
            shifted = jnp.where(shifted < 0.0, shifted + total, shifted)
        distance = shifted + start - middle
        inside = (shifted >= 0.0) & (shifted < span)
        profile = jnp.where(inside, jnp.exp(-(distance * distance) / (2.0 * width * width)), 0.0)
        return profile, profile * (-distance / (width * width))

    def chunk(number, carry):
        rows = lax.broadcasted_iota(jnp.int32, (LANES, plan.atoms), 0) + number * LANES
        onehot = (place[...] == rows).astype(jnp.float32)
        ordered = lax.dot_general(
            table,
            onehot,
            (((1,), (1,)), ((), ())),
            precision=highest,
            preferred_element_type=jnp.float32,
        )
        row = [ordered[k : k + 1, :] for k in range(10)]
        depth = lax.broadcasted_iota(jnp.int32, (plan.total_z, LANES), 0) + ax * plan.cells_z
        depth = jnp.where(depth >= plan.total_z, depth - plan.total_z, depth).astype(jnp.float32)
        profile, slope = pair(
            depth, row[2] * plan.cells_z, row[5] * plan.cells_z, row[8], width_z, plan.total_z
        )
        z_out[number, :, :LANES] = profile
        z_out[number, :, LANES:] = slope
        spot = lax.broadcasted_iota(jnp.int32, (plan.ring, LANES), 0)
        spot = jnp.where(spot < plan.cells_a + 4, spot, spot - plan.ring) + ang * plan.cells_a
        spot = jnp.where(spot < 0, spot + plan.total_a, spot)
        spot = jnp.where(spot >= plan.total_a, spot - plan.total_a, spot).astype(jnp.float32)
        profile, slope = pair(
            spot, row[1] * plan.cells_a, row[4] * plan.cells_a, row[7], width_a, plan.total_a
        )
        a_out[number, 0] = profile
        a_out[number, 1] = slope
        slot = lax.broadcasted_iota(jnp.int32, (plan.slots, LANES), 0)
        level = slot
        for side in range(plan.sides):
            first = plan.cells_r + SWEEPS * side
            level = jnp.where(slot >= first, plan.side_row(side, rad, slot - first + 1), level)
        level = (level + rad * plan.cells_r).astype(jnp.float32)
        profile, slope = pair(
            level, row[0] * plan.cells_r, row[3] * plan.cells_r, row[6], width_r, None
        )
        radius = 0.5 * plan.total_r + level + 0.5
        strength = row[9] * amplitude
        r_out[number, 0] = strength * (plan.angle_step * radius) * slope
        r_out[number, 1] = strength * profile
        r_out[number, 2] = strength * (plan.angle_step * radius) * profile
        return carry

    if plan.chunks == 1:
        chunk(0, 0)
    else:
        lax.fori_loop(0, plan.chunks, chunk, 0)
    for copy in copies[5:]:
        copy.wait()


def sweeps_kernel(
    plan,
    pot_own,
    pot_other,
    rho_own,
    rho_other,
    z_fac,
    a_fac,
    r_fac,
    own_out,
    hal_out,
    rad_out,
    first,
    second,
    grown,
    coef,
):
    rad = lax.axis_index("rad")
    guard, rows, ring, depth = plan.guard, plan.cells_r, plan.ring, plan.total_z
    weights = sweep_weights(SWEEPS)

    level = lax.broadcasted_iota(jnp.int32, (coef.shape[1], depth), 0) - guard + rad * rows
    valid = (level >= 0) & (level < plan.total_r)
    radius = 0.5 * plan.total_r + level.astype(jnp.float32) + 0.5
    upper, lower = (radius + 0.5) / radius, (radius - 0.5) / radius
    angular = 1.0 / (radius * radius * (plan.angle_step * plan.angle_step))
    diagonal = upper + lower + 2.0 * angular + 2.0
    inverse = jnp.where(valid, 1.0 / diagonal, 0.0)
    coef[0] = upper
    coef[1] = lower
    coef[2] = angular
    coef[3] = inverse

    blank = jnp.zeros((ring, depth), jnp.float32)
    for buffer in (first, second):
        for row in range(guard):
            buffer[row] = blank
            buffer[guard + rows + row] = blank
    tail = jnp.zeros((ring - plan.cells_a, depth), jnp.float32)

    def whole(own, other, row):
        return jnp.concatenate([jnp.concatenate([own[row], other[row]], axis=1), tail], axis=0)

    for row in range(rows):
        first[guard + row] = whole(pot_own, pot_other, row)

    def relaxed(source, row, weight, charge):
        center = source[row]
        up, down, turn, inverse = (coef[k, pl.ds(row, 1), :] for k in range(4))
        total = pltpu.roll(center, 1, 1) + pltpu.roll(center, depth - 1, 1)
        total += turn * (pltpu.roll(center, 1, 0) + pltpu.roll(center, ring - 1, 0))
        total += up * source[row + 1] + down * source[row - 1]
        if charge is not None:
            total += charge
        return (1.0 - weight) * center + (weight * inverse) * total

    def send_row(slot, fresh):
        tiles = ring // 8
        for tile in range(tiles - 1):
            rad_out[slot * tiles + tile] = fresh[8 * tile : 8 * tile + 8, plan.cells_z :]
        rad_out[slot * tiles + tiles - 1] = fresh[plan.cells_a :, : plan.cells_z]

    source, target = first, second
    for sweep in range(SWEEPS):
        last = sweep == SWEEPS - 1
        for row in range(rows):
            fresh = relaxed(source, guard + row, weights[sweep], whole(rho_own, rho_other, row))
            if last:
                grown[row] = fresh
                own_out[row] = fresh[: plan.cells_a, : plan.cells_z]
                hal_out[row] = fresh[plan.cells_a :, plan.cells_z :]
            else:
                target[guard + row] = fresh
        for side in range(plan.sides):
            for step in range(1, sweep + 2):
                place = guard + plan.side_row(side, rad, step)
                fresh = relaxed(source, place, weights[sweep], None)
                if last:
                    slot = SWEEPS * side + step - 1
                    grown[rows + slot] = fresh
                    send_row(slot, fresh)
                else:
                    target[place] = fresh
        source, target = target, source

    force_base = plan.side_tiles

    def chunk(number, carry):
        spread = jnp.dot(
            grown[...].reshape(plan.slots * ring, depth),
            z_fac[number],
            precision=highest,
            preferred_element_type=jnp.float32,
        )
        sums = [jnp.zeros((ring, LANES), jnp.float32) for _ in range(3)]
        for slot in range(plan.slots):
            piece = spread[slot * ring : (slot + 1) * ring]
            for k, part in enumerate((piece[:, :LANES], piece[:, :LANES], piece[:, LANES:])):
                sums[k] += r_fac[number, k, pl.ds(slot, 1), :] * part
        total = [
            jnp.sum(a_fac[number, turn] * sums[k], axis=0, keepdims=True)
            for k, turn in enumerate((0, 1, 0))
        ]
        total.append(jnp.zeros((5, LANES), jnp.float32))
        rad_out[force_base + number] = jnp.concatenate(total, axis=0)
        return carry

    if plan.chunks == 1:
        chunk(0, 0)
    else:
        lax.fori_loop(0, plan.chunks, chunk, 0)


def turn_kernel(plan, *refs):
    hal, landed, forces = refs[0], refs[1 : 1 + plan.sides], refs[1 + plan.sides : -3]
    even_out, odd_out, held = refs[-3:]
    rad, ang = lax.axis_index("rad"), lax.axis_index("ang")
    width = plan.cells_z
    held[...] = hal[...]
    tiles = plan.ring // 8
    for side in range(plan.sides):
        for step in range(1, SWEEPS + 1):
            row = plan.landing_row(side, rad, step)
            held[row] = held[row] + landed[side][step * tiles - 1]
    low_half = lax.broadcasted_iota(jnp.int32, (8, width), 0) < 4
    is_even = (lax.broadcasted_iota(jnp.int32, (8, width), 0) * 0 + ang) % 2 == 0
    pairs = plan.cells_r // 2
    for tile in range(pairs):
        front, back = held[2 * tile], held[2 * tile + 1]
        above = jnp.where(low_half, front, pltpu.roll(back, 4, 0))
        below = jnp.where(low_half, pltpu.roll(front, 4, 0), back)
        even_out[tile] = jnp.where(is_even, above, below)
        odd_out[tile] = jnp.where(is_even, below, above)
    for number in range(plan.chunks):
        total = forces[0][number - plan.chunks + forces[0].shape[0]]
        if len(forces) > 1:
            total = total + forces[1][number - plan.chunks + forces[1].shape[0]]
        even_out[pairs + number] = total


def final_kernel(plan, *refs):
    own, landed, even_in, odd_in, out = refs[0], refs[1 : 1 + plan.sides], *refs[-3:]
    rad, ang = lax.axis_index("rad"), lax.axis_index("ang")
    width = plan.cells_z
    low_half = lax.broadcasted_iota(jnp.int32, (8, width), 0) < 4
    is_even = (lax.broadcasted_iota(jnp.int32, (8, width), 0) * 0 + ang) % 2 == 0
    top = plan.cells_a - 8
    tiles = plan.ring // 8
    for tile in range(plan.cells_r // 2):
        even, odd = even_in[tile], odd_in[tile]
        above, below = jnp.where(is_even, even, odd), jnp.where(is_even, odd, even)
        for half in range(2):
            row = 2 * tile + half
            from_below = below if half == 0 else pltpu.roll(below, 4, 0)
            from_above = above if half == 1 else pltpu.roll(above, 4, 0)
            out[row] = own[row]
            out[row, 0:8, :] += jnp.where(low_half, from_below, 0.0)
            out[row, top:, :] += jnp.where(low_half, 0.0, from_above)
    for side in range(plan.sides):
        for step in range(1, SWEEPS + 1):
            row = plan.landing_row(side, rad, step)
            for tile in range(tiles - 1):
                out[row, 8 * tile : 8 * tile + 8, :] += landed[side][(step - 1) * tiles + tile]


def call(kernel, plan, outs, scratch, flops, bytes_moved, args, spaces=None, megabytes=24):
    in_vmem = pl.BlockSpec(memory_space=pltpu.VMEM)
    return pl.pallas_call(
        functools.partial(kernel, plan),
        out_shape=[jax.ShapeDtypeStruct(shape, jnp.float32) for shape in outs],
        in_specs=spaces or [in_vmem] * len(args),
        out_specs=[in_vmem] * len(outs),
        scratch_shapes=scratch,
        compiler_params=pltpu.CompilerParams(vmem_limit_bytes=megabytes * 2**20),
        cost_estimate=pl.CostEstimate(flops=flops, bytes_accessed=bytes_moved, transcendentals=0),
    )(*args)


def shards(plan, potential, density, anchor, extent, center, charge, place):
    ring, depth, slots, chunks = plan.ring, plan.total_z, plan.slots, plan.chunks
    rows, width, block = plan.cells_r, plan.cells_z, potential.shape
    swap = [(0, 1), (1, 0)]
    potential_other = lax.ppermute(potential, "ax", swap)
    density_other = lax.ppermute(density, "ax", swap)
    tables = (anchor, extent, center, charge.reshape(1, -1), place.reshape(1, -1))
    *factors, potential, density = call(
        factors_kernel,
        plan,
        [(chunks, depth, 2 * LANES), (chunks, 2, ring, LANES), (chunks, 3, slots, LANES)] + [block] * 2,
        [pltpu.VMEM(table.shape, table.dtype) for table in tables] + [pltpu.SemaphoreType.DMA((7,))],
        10**6,
        10**6,
        [pltpu.with_memory_space_constraint(value, pltpu.HBM) for value in (*tables, potential, density)],
        [pl.BlockSpec(memory_space=pl.ANY)] * 7,
    )
    tall = rows + 2 * plan.guard
    scratch = [(tall, ring, depth)] * 2 + [(slots, ring, depth), (4, tall, depth)]
    own, hal, sides = call(
        sweeps_kernel,
        plan,
        [block, (rows, 8, width), (plan.side_tiles + chunks, 8, LANES)],
        [pltpu.VMEM(shape, jnp.float32) for shape in scratch],
        10**9,
        10**7,
        (potential, potential_other, density, density_other, *factors),
    )

    def send(value, move):
        return lax.ppermute(value, AXES, plan.moves(move))

    per_side = plan.side_tiles // max(1, plan.sides)
    if plan.sides == 1:
        landed = [send(sides, lambda r, a: (1 - r, a))]
        forces = [sides, landed[0]]
    else:
        landed = []
        force = sides[plan.side_tiles :]
        if plan.sides == 2:
            landed.append(send(sides[per_side : 2 * per_side], lambda r, a: (r - 1, a) if r else None))
            last = plan.n_rad - 1
            landed.append(send(sides[:per_side], lambda r, a: (r + 1, a) if r < last else None))
        step = 1
        while step < plan.n_rad:
            force = force + send(force, lambda r, a: (r ^ step, a))
            step *= 2
        forces = [force]
    pairs = rows // 2
    even, odd = call(
        turn_kernel,
        plan,
        [(pairs + chunks, 8, width), (pairs, 8, width)],
        [pltpu.VMEM((rows, 8, width), jnp.float32)],
        10**5,
        10**6,
        (hal, *landed, *forces),
    )
    odd_in = send(odd, lambda r, a: (r, (a + 1 - 2 * (1 - a % 2)) % plan.n_ang))
    even_in = send(even, lambda r, a: (r, a ^ 1))
    force = even[pairs:] + even_in[pairs:]
    step = 2
    while step < plan.n_ang:
        force = force + send(force, lambda r, a: (r, a ^ step))
        step *= 2
    (final,) = call(
        final_kernel, plan, [block], [], 10**5, 10**6, (own, *landed, even_in, odd_in)
    )
    share = plan.atoms // (plan.n_rad * plan.n_ang * plan.n_ax)
    first = plan.device(*(lax.axis_index(name) for name in AXES)) * share
    mine = lax.dynamic_slice(force, (first // LANES, 0, first % LANES), (1, 3, share))
    return final, mine.reshape(3, share)


def solution(mesh):
    whole = P("rad", "ang", "ax")

    def run(potential, density, anchor, extent, center, charge, place):
        sizes = [mesh.shape[name] for name in AXES]
        block = [total // parts for total, parts in zip(potential.shape, sizes)]
        plan = Plan(mesh, block, charge.shape[0])
        return jax.shard_map(
            functools.partial(shards, plan),
            mesh=mesh,
            in_specs=(whole, whole, P(), P(), P(), P(), P()),
            out_specs=(whole, P(None, AXES)),
            check_vma=False,
        )(potential, density, anchor, extent, center, charge, place)

    return run
```

```python
import functools
import math

import jax
import jax.numpy as jnp
from jax import lax
from jax.experimental import pallas as pl
from jax.experimental.pallas import tpu as pltpu
from jax.sharding import PartitionSpec as P

SWEEPS = 3
LANES = 128
AXES = ("rad", "ang", "ax")

cheb_low = 0.2
cheb_high = 2.0
highest = lax.Precision.HIGHEST


def sweep_weights(total_sweeps):
    middle = 0.5 * (cheb_high + cheb_low)
    spread = 0.5 * (cheb_high - cheb_low)
    return [
        1.0 / (middle + spread * math.cos(math.pi * (2 * number + 1) / (2 * total_sweeps)))
        for number in range(total_sweeps)
    ]


class Plan:
    def __init__(self, mesh, block, atoms):
        self.n_rad, self.n_ang, self.n_ax = (mesh.shape[name] for name in AXES)
        self.cells_r, self.cells_a, self.cells_z = block
        self.atoms = atoms
        self.chunks = atoms // LANES
        self.ring = self.cells_a + 8
        self.total_r = self.cells_r * self.n_rad
        self.total_a = self.cells_a * self.n_ang
        self.total_z = self.cells_z * self.n_ax
        self.angle_step = 2.0 * math.pi / self.total_a
        self.sides = 0 if self.n_rad == 1 else 1 if self.n_rad == 2 else 2
        self.slots = self.cells_r + SWEEPS * self.sides
        self.guard = SWEEPS + 1
        self.beyond = SWEEPS * self.sides
        self.face = SWEEPS * (self.cells_a // 8)
        self.halo = (self.slots + 1) // 2

    def sign(self, side, rad):
        if self.sides == 1:
            return 1 - 2 * rad
        return 1 - 2 * side

    def side_row(self, side, rad, step):
        sign = self.sign(side, rad)
        return (self.cells_r - 1) * (1 + sign) // 2 + sign * step

    def landing_row(self, side, rad, step):
        sign = self.sign(side, rad)
        return (self.cells_r - 1) * (1 + sign) // 2 - sign * (step - 1)

    def device(self, rad, ang, ax):
        return (rad * self.n_ang + ang) * self.n_ax + ax

    def moves(self, move):
        found = []
        for rad in range(self.n_rad):
            for ang in range(self.n_ang):
                target = move(rad, ang)
                if target is not None:
                    for ax in range(self.n_ax):
                        found.append((self.device(rad, ang, ax), self.device(*target, 1 - ax)))
        return found


def even_sector(ang):
    return (lax.broadcasted_iota(jnp.int32, (8, LANES), 0) * 0 + ang) % 2 == 0


def pack(front, back, is_even):
    low_half = lax.broadcasted_iota(jnp.int32, front.shape, 0) < 4
    above = jnp.where(low_half, front, pltpu.roll(back, 4, 0))
    below = jnp.where(low_half, pltpu.roll(front, 4, 0), back)
    return jnp.where(is_even, above, below), jnp.where(is_even, below, above)


def unpack(even, odd, half, is_even):
    low_half = lax.broadcasted_iota(jnp.int32, even.shape, 0) < 4
    above, below = jnp.where(is_even, even, odd), jnp.where(is_even, odd, even)
    first = below if half == 0 else pltpu.roll(below, 4, 0)
    last = above if half == 1 else pltpu.roll(above, 4, 0)
    return jnp.where(low_half, first, 0.0), jnp.where(low_half, 0.0, last)


def factors_kernel(plan, *refs):
    sources, (z_out, a_out, r_out, pot_out, rho_out), held = refs[:7], refs[7:12], refs[12:17]
    copies = [
        pltpu.make_async_copy(source, target, refs[17].at[k])
        for k, (source, target) in enumerate(zip(sources, (*held, pot_out, rho_out)))
    ]
    for copy in copies:
        copy.start()
    for copy in copies[:5]:
        copy.wait()
    anchor, extent, center, charge, place = held
    rad, ang, ax = (lax.axis_index(name) for name in AXES)
    width_r, width_a, width_z = plan.cells_r / 3.0, plan.cells_a / 3.0, plan.cells_z / 3.0
    amplitude = 1.0 / math.sqrt(width_a * width_z / width_r)
    table = jnp.concatenate(
        [
            anchor[...].astype(jnp.float32),
            extent[...].astype(jnp.float32),
            center[...],
            charge[...],
            jnp.zeros((6, plan.atoms), jnp.float32),
        ],
        axis=0,
    )

    def pair(cell, start, span, middle, width, total):
        shifted = cell - start
        if total is not None:
            shifted = jnp.where(shifted < 0.0, shifted + total, shifted)
        distance = shifted + start - middle
        inside = (shifted >= 0.0) & (shifted < span)
        profile = jnp.where(inside, jnp.exp(-(distance * distance) / (2.0 * width * width)), 0.0)
        return profile, profile * (-distance / (width * width))

    def chunk(number, carry):
        rows = lax.broadcasted_iota(jnp.int32, (LANES, plan.atoms), 0) + number * LANES
        onehot = (place[...] == rows).astype(jnp.float32)
        ordered = lax.dot_general(
            table,
            onehot,
            (((1,), (1,)), ((), ())),
            precision=highest,
            preferred_element_type=jnp.float32,
        )
        row = [ordered[k : k + 1, :] for k in range(10)]
        depth = lax.broadcasted_iota(jnp.int32, (plan.total_z, LANES), 0) + ax * plan.cells_z
        depth = jnp.where(depth >= plan.total_z, depth - plan.total_z, depth).astype(jnp.float32)
        profile, slope = pair(
            depth, row[2] * plan.cells_z, row[5] * plan.cells_z, row[8], width_z, plan.total_z
        )
        z_out[number, :, :LANES] = profile
        z_out[number, :, LANES:] = slope
        spot = lax.broadcasted_iota(jnp.int32, (plan.ring, LANES), 0)
        spot = jnp.where(spot < plan.cells_a + 4, spot, spot - plan.ring) + ang * plan.cells_a
        spot = jnp.where(spot < 0, spot + plan.total_a, spot)
        spot = jnp.where(spot >= plan.total_a, spot - plan.total_a, spot).astype(jnp.float32)
        profile, slope = pair(
            spot, row[1] * plan.cells_a, row[4] * plan.cells_a, row[7], width_a, plan.total_a
        )
        a_out[number, 0] = profile
        a_out[number, 1] = slope
        slot = lax.broadcasted_iota(jnp.int32, (plan.slots, LANES), 0)
        level = slot
        for side in range(plan.sides):
            first = plan.cells_r + SWEEPS * side
            level = jnp.where(slot >= first, plan.side_row(side, rad, slot - first + 1), level)
        level = (level + rad * plan.cells_r).astype(jnp.float32)
        profile, slope = pair(
            level, row[0] * plan.cells_r, row[3] * plan.cells_r, row[6], width_r, None
        )
        radius = 0.5 * plan.total_r + level + 0.5
        strength = row[9] * amplitude
        r_out[number, 0] = strength * (plan.angle_step * radius) * slope
        r_out[number, 1] = strength * profile
        r_out[number, 2] = strength * (plan.angle_step * radius) * profile
        return carry

    if plan.chunks == 1:
        chunk(0, 0)
    else:
        lax.fori_loop(0, plan.chunks, chunk, 0)
    for copy in copies[5:]:
        copy.wait()


def sweeps_kernel(
    plan,
    pot_own,
    pot_other,
    rho_own,
    rho_other,
    z_fac,
    a_fac,
    r_fac,
    own_out,
    even_out,
    odd_out,
    face_out,
    force_out,
    first,
    second,
    grown,
    coef,
):
    rad = lax.axis_index("rad")
    guard, rows, ring, depth = plan.guard, plan.cells_r, plan.ring, plan.total_z
    weights = sweep_weights(SWEEPS)

    level = lax.broadcasted_iota(jnp.int32, (coef.shape[1], depth), 0) - guard + rad * rows
    valid = (level >= 0) & (level < plan.total_r)
    radius = 0.5 * plan.total_r + level.astype(jnp.float32) + 0.5
    upper, lower = (radius + 0.5) / radius, (radius - 0.5) / radius
    angular = 1.0 / (radius * radius * (plan.angle_step * plan.angle_step))
    diagonal = upper + lower + 2.0 * angular + 2.0
    inverse = jnp.where(valid, 1.0 / diagonal, 0.0)
    coef[0] = upper
    coef[1] = lower
    coef[2] = angular
    coef[3] = inverse

    blank = jnp.zeros((ring, depth), jnp.float32)
    for buffer in (first, second):
        for row in range(guard):
            buffer[row] = blank
            buffer[guard + rows + row] = blank
    tail = jnp.zeros((ring - plan.cells_a, depth), jnp.float32)

    def whole(own, other, row):
        return jnp.concatenate([jnp.concatenate([own[row], other[row]], axis=1), tail], axis=0)

    for row in range(rows):
        first[guard + row] = whole(pot_own, pot_other, row)

    def relaxed(source, row, weight, charge):
        center = source[row]
        up, down, turn, inverse = (coef[k, pl.ds(row, 1), :] for k in range(4))
        total = pltpu.roll(center, 1, 1) + pltpu.roll(center, depth - 1, 1)
        total += turn * (pltpu.roll(center, 1, 0) + pltpu.roll(center, ring - 1, 0))
        total += up * source[row + 1] + down * source[row - 1]
        if charge is not None:
            total += charge
        return (1.0 - weight) * center + (weight * inverse) * total

    def send_row(slot, fresh):
        tiles = plan.cells_a // 8
        for tile in range(tiles):
            face_out[slot * tiles + tile] = fresh[8 * tile : 8 * tile + 8, plan.cells_z :]

    source, target = first, second
    for sweep in range(SWEEPS):
        last = sweep == SWEEPS - 1
        for row in range(rows):
            fresh = relaxed(source, guard + row, weights[sweep], whole(rho_own, rho_other, row))
            if last:
                grown[row] = fresh
                own_out[row] = fresh[: plan.cells_a, : plan.cells_z]
            else:
                target[guard + row] = fresh
        for side in range(plan.sides):
            for step in range(1, sweep + 2):
                place = guard + plan.side_row(side, rad, step)
                fresh = relaxed(source, place, weights[sweep], None)
                if last:
                    slot = SWEEPS * side + step - 1
                    grown[rows + slot] = fresh
                    send_row(slot, fresh)
                else:
                    target[place] = fresh
        source, target = target, source

    is_even = even_sector(lax.axis_index("ang"))
    halo = [grown[slot, plan.cells_a :, plan.cells_z :] for slot in range(rows)]
    halo += [grown[slot, plan.cells_a :, : plan.cells_z] for slot in range(rows, plan.slots)]
    halo += [jnp.zeros_like(halo[0])] * (2 * plan.halo - plan.slots)
    for tile in range(plan.halo):
        even_out[tile], odd_out[tile] = pack(halo[2 * tile], halo[2 * tile + 1], is_even)

    def chunk(number, carry):
        spread = jnp.dot(
            grown[...].reshape(plan.slots * ring, depth),
            z_fac[number],
            precision=highest,
            preferred_element_type=jnp.float32,
        )
        sums = [jnp.zeros((ring, LANES), jnp.float32) for _ in range(3)]
        for slot in range(plan.slots):
            piece = spread[slot * ring : (slot + 1) * ring]
            for k, part in enumerate((piece[:, :LANES], piece[:, :LANES], piece[:, LANES:])):
                sums[k] += r_fac[number, k, pl.ds(slot, 1), :] * part
        total = [
            jnp.sum(a_fac[number, turn] * sums[k], axis=0, keepdims=True)
            for k, turn in enumerate((0, 1, 0))
        ]
        total.append(jnp.zeros((5, LANES), jnp.float32))
        force_out[number] = jnp.concatenate(total, axis=0)
        return carry

    if plan.chunks == 1:
        chunk(0, 0)
    else:
        lax.fori_loop(0, plan.chunks, chunk, 0)


def join_kernel(plan, even, *refs):
    forces, out = refs[:-1], refs[-1]
    out[: plan.halo] = even[...]
    out[plan.halo :] = forces[0][...] if len(forces) == 1 else forces[0][...] + forces[1][...]


def fold_kernel(plan, face, even, even_in, odd_in, face_out, force_out):
    is_even = even_sector(lax.axis_index("ang"))
    face_out[...] = face[...]
    tiles = plan.cells_a // 8
    for slot in range(plan.beyond):
        tile, half = divmod(plan.cells_r + slot, 2)
        first, last = unpack(even_in[tile], odd_in[tile], half, is_even)
        face_out[slot * tiles] = face_out[slot * tiles] + first
        face_out[slot * tiles + tiles - 1] = face_out[slot * tiles + tiles - 1] + last
    force_out[...] = even[plan.halo :] + even_in[plan.halo :]


def add_kernel(plan, first, second, out):
    out[...] = first[...] + second[...]


def copy_kernel(plan, value, after, out):
    out[...] = value[...]


def final_kernel(plan, *refs):
    own, landed, even_in, odd_in, force, out, force_out = refs[0], refs[1 : 1 + plan.sides], *refs[-5:]
    force_out[...] = force[...]
    rad = lax.axis_index("rad")
    is_even = even_sector(lax.axis_index("ang"))
    top = plan.cells_a - 8
    tiles = plan.cells_a // 8
    for row in range(plan.cells_r):
        first, last = unpack(even_in[row // 2], odd_in[row // 2], row % 2, is_even)
        out[row] = own[row]
        out[row, 0:8, :] += first
        out[row, top:, :] += last
    for side in range(plan.sides):
        for step in range(1, SWEEPS + 1):
            row = plan.landing_row(side, rad, step)
            for tile in range(tiles):
                out[row, 8 * tile : 8 * tile + 8, :] += landed[side][(step - 1) * tiles + tile]


def call(kernel, plan, outs, scratch, flops, bytes_moved, args, spaces=None, megabytes=24):
    in_vmem = pl.BlockSpec(memory_space=pltpu.VMEM)
    return pl.pallas_call(
        functools.partial(kernel, plan),
        out_shape=[jax.ShapeDtypeStruct(shape, jnp.float32) for shape in outs],
        in_specs=spaces or [in_vmem] * len(args),
        out_specs=[in_vmem] * len(outs),
        scratch_shapes=scratch,
        compiler_params=pltpu.CompilerParams(vmem_limit_bytes=megabytes * 2**20),
        cost_estimate=pl.CostEstimate(flops=flops, bytes_accessed=bytes_moved, transcendentals=0),
    )(*args)


def shards(plan, potential, density, anchor, extent, center, charge, place):
    ring, depth, slots, chunks = plan.ring, plan.total_z, plan.slots, plan.chunks
    rows, width, block = plan.cells_r, plan.cells_z, potential.shape
    swap = [(0, 1), (1, 0)]
    potential_other = lax.ppermute(potential, "ax", swap)
    density_other = lax.ppermute(density, "ax", swap)
    tables = (anchor, extent, center, charge.reshape(1, -1), place.reshape(1, -1))
    *factors, potential, density = call(
        factors_kernel,
        plan,
        [(chunks, depth, 2 * LANES), (chunks, 2, ring, LANES), (chunks, 3, slots, LANES)] + [block] * 2,
        [pltpu.VMEM(table.shape, table.dtype) for table in tables] + [pltpu.SemaphoreType.DMA((7,))],
        10**6,
        10**6,
        [pltpu.with_memory_space_constraint(value, pltpu.HBM) for value in (*tables, potential, density)],
        [pl.BlockSpec(memory_space=pl.ANY)] * 7,
    )
    tall = rows + 2 * plan.guard
    scratch = [(tall, ring, depth)] * 2 + [(slots, ring, depth), (4, tall, depth)]
    own, even, odd, face, force = call(
        sweeps_kernel,
        plan,
        [block, (plan.halo, 8, width), (plan.halo, 8, width)]
        + [(max(1, plan.face * plan.sides), 8, width), (chunks, 8, LANES)],
        [pltpu.VMEM(shape, jnp.float32) for shape in scratch],
        10**9,
        10**7,
        (potential, potential_other, density, density_other, *factors),
    )

    def send(value, move):
        return lax.ppermute(value, AXES, plan.moves(move))

    def send_radial(value, length):
        if plan.sides == 0:
            return []
        if plan.sides == 1:
            return [send(value, lambda r, a: (1 - r, a))]
        last = plan.n_rad - 1
        return [
            send(value[length : 2 * length], lambda r, a: (r - 1, a) if r else None),
            send(value[:length], lambda r, a: (r + 1, a) if r < last else None),
        ]

    def send_angular(value, step):
        return send(value, lambda r, a: (r, a ^ step))

    (odd,) = call(copy_kernel, plan, [odd.shape], [], 10**6, 10**6, (odd, force))
    odd_in = send(odd, lambda r, a: (r, (a + 1 - 2 * (1 - a % 2)) % plan.n_ang))
    parts = [force]
    step = plan.n_ang // 2
    while step > 2:
        force = sum(parts)
        parts = [force, send_angular(force, step)]
        step //= 2
    (even,) = call(
        join_kernel, plan, [(plan.halo + chunks, 8, width)], [], 10**9, 10**9, (even, *parts)
    )
    even_in = send_angular(even, 1)
    (odd_in,) = call(copy_kernel, plan, [odd.shape], [], 10**9, 10**9, (odd_in, odd))
    face, force = call(
        fold_kernel,
        plan,
        [face.shape, (chunks, 8, LANES)],
        [],
        10**5,
        10**5,
        (face, even, even_in, odd_in),
    )
    (face,) = call(copy_kernel, plan, [face.shape], [], 10**6, 10**6, (face, force))
    faces = send_radial(face, plan.face)
    step = 1
    while step < plan.n_rad:
        part = send(force, lambda r, a: (r ^ step, a))
        (force,) = call(add_kernel, plan, [force.shape], [], 10**9, 10**9, (force, part))
        step *= 2
    last_part = send_angular(force, 2) if plan.n_ang > 2 else jnp.zeros_like(force)
    final, force = call(
        final_kernel,
        plan,
        [block, force.shape],
        [],
        10**5,
        10**6,
        (own, *faces, even_in, odd_in, force),
    )
    force = force + last_part
    share = plan.atoms // (plan.n_rad * plan.n_ang * plan.n_ax)
    first = plan.device(*(lax.axis_index(name) for name in AXES)) * share
    mine = lax.dynamic_slice(force, (first // LANES, 0, first % LANES), (1, 3, share))
    return final, mine.reshape(3, share)


def solution(mesh):
    whole = P("rad", "ang", "ax")

    def run(potential, density, anchor, extent, center, charge, place):
        sizes = [mesh.shape[name] for name in AXES]
        block = [total // parts for total, parts in zip(potential.shape, sizes)]
        plan = Plan(mesh, block, charge.shape[0])
        return jax.shard_map(
            functools.partial(shards, plan),
            mesh=mesh,
            in_specs=(whole, whole, P(), P(), P(), P(), P()),
            out_specs=(whole, P(None, AXES)),
            check_vma=False,
        )(potential, density, anchor, extent, center, charge, place)

    return run
```

```python
import functools
import math

import jax
import jax.numpy as jnp
from jax import lax
from jax.experimental import pallas as pl
from jax.experimental.pallas import tpu as pltpu
from jax.sharding import PartitionSpec as P

SWEEPS = 3
LANES = 128
AXES = ("rad", "ang", "ax")

cheb_low = 0.2
cheb_high = 2.0
highest = lax.Precision.HIGHEST


def sweep_weights(total_sweeps):
    middle = 0.5 * (cheb_high + cheb_low)
    spread = 0.5 * (cheb_high - cheb_low)
    return [
        1.0 / (middle + spread * math.cos(math.pi * (2 * number + 1) / (2 * total_sweeps)))
        for number in range(total_sweeps)
    ]


class Plan:
    def __init__(self, mesh, block, atoms):
        self.n_rad, self.n_ang, self.n_ax = (mesh.shape[name] for name in AXES)
        self.cells_r, self.cells_a, self.cells_z = block
        self.atoms = atoms
        self.chunks = atoms // LANES
        self.ring = self.cells_a + 8
        self.total_r = self.cells_r * self.n_rad
        self.total_a = self.cells_a * self.n_ang
        self.total_z = self.cells_z * self.n_ax
        self.angle_step = 2.0 * math.pi / self.total_a
        self.sides = 0 if self.n_rad == 1 else 1 if self.n_rad == 2 else 2
        self.slots = self.cells_r + SWEEPS * self.sides
        self.guard = SWEEPS + 1
        self.beyond = SWEEPS * self.sides
        self.tiles = self.cells_a // 8
        self.halo = (self.slots + 1) // 2

    def sign(self, side, rad):
        if self.sides == 1:
            return 1 - 2 * rad
        return 1 - 2 * side

    def side_row(self, side, rad, step):
        sign = self.sign(side, rad)
        return (self.cells_r - 1) * (1 + sign) // 2 + sign * step

    def landing_row(self, side, rad, step):
        sign = self.sign(side, rad)
        return (self.cells_r - 1) * (1 + sign) // 2 - sign * (step - 1)

    def device(self, rad, ang, ax):
        return (rad * self.n_ang + ang) * self.n_ax + ax

    def moves(self, move):
        found = []
        for rad in range(self.n_rad):
            for ang in range(self.n_ang):
                target = move(rad, ang)
                if target is not None:
                    for ax in range(self.n_ax):
                        found.append((self.device(rad, ang, ax), self.device(*target, 1 - ax)))
        return found


def even_sector(ang):
    return (lax.broadcasted_iota(jnp.int32, (8, LANES), 0) * 0 + ang) % 2 == 0


def pack(front, back, is_even):
    low_half = lax.broadcasted_iota(jnp.int32, front.shape, 0) < 4
    above = jnp.where(low_half, front, pltpu.roll(back, 4, 0))
    below = jnp.where(low_half, pltpu.roll(front, 4, 0), back)
    return jnp.where(is_even, above, below), jnp.where(is_even, below, above)


def unpack(even, odd, half, is_even):
    low_half = lax.broadcasted_iota(jnp.int32, even.shape, 0) < 4
    above, below = jnp.where(is_even, even, odd), jnp.where(is_even, odd, even)
    first = below if half == 0 else pltpu.roll(below, 4, 0)
    last = above if half == 1 else pltpu.roll(above, 4, 0)
    return jnp.where(low_half, first, 0.0), jnp.where(low_half, 0.0, last)


def factors_kernel(plan, *refs):
    sources, outs, held = refs[:7], refs[7:14], refs[14:19]
    z_high, z_low, a_out, r_out, coef, pot_out, rho_out = outs
    copies = [
        pltpu.make_async_copy(source, target, refs[19].at[k])
        for k, (source, target) in enumerate(zip(sources, (*held, pot_out, rho_out)))
    ]
    for copy in copies:
        copy.start()
    rad, ang, ax = (lax.axis_index(name) for name in AXES)
    level = lax.broadcasted_iota(jnp.int32, coef.shape[1:], 0) - plan.guard + rad * plan.cells_r
    valid = (level >= 0) & (level < plan.total_r)
    radius = 0.5 * plan.total_r + level.astype(jnp.float32) + 0.5
    upper, lower = (radius + 0.5) / radius, (radius - 0.5) / radius
    angular = 1.0 / (radius * radius * (plan.angle_step * plan.angle_step))
    diagonal = upper + lower + 2.0 * angular + 2.0
    inverse = jnp.where(valid, 1.0 / diagonal, 0.0)
    coef[0] = upper
    coef[1] = lower
    coef[2] = angular
    coef[3] = inverse

    for copy in copies[:5]:
        copy.wait()
    anchor, extent, center, charge, place = held
    width_r, width_a, width_z = plan.cells_r / 3.0, plan.cells_a / 3.0, plan.cells_z / 3.0
    amplitude = 1.0 / math.sqrt(width_a * width_z / width_r)
    table = jnp.concatenate(
        [
            anchor[...].astype(jnp.float32),
            extent[...].astype(jnp.float32),
            center[...],
            charge[...],
            jnp.zeros((6, plan.atoms), jnp.float32),
        ],
        axis=0,
    )

    def pair(cell, start, span, middle, width, total):
        shifted = cell - start
        if total is not None:
            shifted = jnp.where(shifted < 0.0, shifted + total, shifted)
        distance = shifted + start - middle
        inside = (shifted >= 0.0) & (shifted < span)
        profile = jnp.where(inside, jnp.exp(-(distance * distance) / (2.0 * width * width)), 0.0)
        return profile, profile * (-distance / (width * width))

    def chunk(number, carry):
        rows = lax.broadcasted_iota(jnp.int32, (LANES, plan.atoms), 0) + number * LANES
        onehot = (place[...] == rows).astype(jnp.float32)
        ordered = lax.dot_general(
            table,
            onehot,
            (((1,), (1,)), ((), ())),
            precision=highest,
            preferred_element_type=jnp.float32,
        )
        row = [ordered[k : k + 1, :] for k in range(10)]
        depth = lax.broadcasted_iota(jnp.int32, (plan.total_z, LANES), 0) + ax * plan.cells_z
        depth = jnp.where(depth >= plan.total_z, depth - plan.total_z, depth).astype(jnp.float32)
        profile, slope = pair(
            depth, row[2] * plan.cells_z, row[5] * plan.cells_z, row[8], width_z, plan.total_z
        )
        factor = jnp.concatenate([profile, slope], axis=1)
        high = factor.astype(jnp.bfloat16)
        z_high[number] = high
        z_low[number] = (factor - high.astype(jnp.float32)).astype(jnp.bfloat16)
        spot = lax.broadcasted_iota(jnp.int32, (plan.ring, LANES), 0)
        spot = jnp.where(spot < plan.cells_a + 4, spot, spot - plan.ring) + ang * plan.cells_a
        spot = jnp.where(spot < 0, spot + plan.total_a, spot)
        spot = jnp.where(spot >= plan.total_a, spot - plan.total_a, spot).astype(jnp.float32)
        profile, slope = pair(
            spot, row[1] * plan.cells_a, row[4] * plan.cells_a, row[7], width_a, plan.total_a
        )
        a_out[number, 0] = profile
        a_out[number, 1] = slope
        slot = lax.broadcasted_iota(jnp.int32, (plan.slots, LANES), 0)
        level = slot
        for side in range(plan.sides):
            first = plan.cells_r + SWEEPS * side
            level = jnp.where(slot >= first, plan.side_row(side, rad, slot - first + 1), level)
        level = (level + rad * plan.cells_r).astype(jnp.float32)
        profile, slope = pair(
            level, row[0] * plan.cells_r, row[3] * plan.cells_r, row[6], width_r, None
        )
        radius = 0.5 * plan.total_r + level + 0.5
        strength = row[9] * amplitude
        r_out[number, 0] = strength * (plan.angle_step * radius) * slope
        r_out[number, 1] = strength * profile
        r_out[number, 2] = strength * (plan.angle_step * radius) * profile
        return carry

    if plan.chunks == 1:
        chunk(0, 0)
    else:
        lax.fori_loop(0, plan.chunks, chunk, 0)
    for copy in copies[5:]:
        copy.wait()


def whole(plan, own, other, row):
    blank = jnp.zeros((plan.ring - plan.cells_a, plan.total_z), jnp.float32)
    return jnp.concatenate([jnp.concatenate([own[row], other[row]], axis=1), blank], axis=0)


def around(plan, center, turn):
    total = pltpu.roll(center, 1, 1) + pltpu.roll(center, plan.total_z - 1, 1)
    return total + turn * (pltpu.roll(center, 1, 0) + pltpu.roll(center, plan.ring - 1, 0))


def start_kernel(plan, pot_own, pot_other, coef, out):
    rad = lax.axis_index("rad")
    rows, weight = plan.cells_r, sweep_weights(SWEEPS)[0]
    plane = functools.partial(whole, plan, pot_own, pot_other)
    for row in range(rows):
        up, down, turn, inverse = (coef[k, pl.ds(plan.guard + row, 1), :] for k in range(4))
        center = plane(row)
        total = around(plan, center, turn)
        if row + 1 < rows:
            total += up * plane(row + 1)
        if row > 0:
            total += down * plane(row - 1)
        out[row] = (1.0 - weight) * center + (weight * inverse) * total
    for side in range(plan.sides):
        place = plan.guard + plan.side_row(side, rad, 1)
        up, down, _, inverse = (coef[k, pl.ds(place, 1), :] for k in range(4))
        factor = jnp.where(plan.sign(side, rad) > 0, down, up)
        out[rows + side] = (weight * inverse * factor) * plane(plan.side_row(side, rad, 0))


def sweeps_kernel(
    plan,
    begun,
    rho_own,
    rho_other,
    coef,
    z_high,
    z_low,
    a_fac,
    r_fac,
    own_out,
    even_out,
    odd_out,
    mid_out,
    edge_out,
    force_out,
    first,
    second,
    grown,
):
    rad = lax.axis_index("rad")
    guard, rows, ring, depth = plan.guard, plan.cells_r, plan.ring, plan.total_z
    weights = sweep_weights(SWEEPS)

    blank = jnp.zeros((ring, depth), jnp.float32)
    for buffer in (first, second):
        for row in range(guard):
            buffer[row] = blank
            buffer[guard + rows + row] = blank
    for row in range(rows):
        inverse = coef[3, pl.ds(guard + row, 1), :]
        charge = whole(plan, rho_own, rho_other, row)
        first[guard + row] = begun[row] + (weights[0] * inverse) * charge
    for side in range(plan.sides):
        first[guard + plan.side_row(side, rad, 1)] = begun[rows + side]
    for slot in range(plan.slots, grown.shape[0]):
        grown[slot] = blank

    def relaxed(source, row, weight, charge):
        center = source[row]
        up, down, turn, inverse = (coef[k, pl.ds(row, 1), :] for k in range(4))
        total = around(plan, center, turn)
        total += up * source[row + 1] + down * source[row - 1]
        if charge is not None:
            total += charge
        return (1.0 - weight) * center + (weight * inverse) * total

    def send_row(slot, fresh):
        part = [fresh[8 * tile : 8 * tile + 8, plan.cells_z :] for tile in range(plan.tiles)]
        edge_out[2 * slot], edge_out[2 * slot + 1] = part[0], part[-1]
        for tile in range(1, plan.tiles - 1):
            mid_out[slot * (plan.tiles - 2) + tile - 1] = part[tile]

    source, target = first, second
    for sweep in range(1, SWEEPS):
        last = sweep == SWEEPS - 1
        for row in range(rows):
            fresh = relaxed(source, guard + row, weights[sweep], whole(plan, rho_own, rho_other, row))
            if last:
                grown[row] = fresh
                own_out[row] = fresh[: plan.cells_a, : plan.cells_z]
            else:
                target[guard + row] = fresh
        for side in range(plan.sides):
            for step in range(1, sweep + 2):
                place = guard + plan.side_row(side, rad, step)
                fresh = relaxed(source, place, weights[sweep], None)
                if last:
                    slot = SWEEPS * side + step - 1
                    grown[rows + slot] = fresh
                    send_row(slot, fresh)
                else:
                    target[place] = fresh
        source, target = target, source

    is_even = even_sector(lax.axis_index("ang"))
    halo = [grown[slot, plan.cells_a :, plan.cells_z :] for slot in range(rows)]
    halo += [grown[slot, plan.cells_a :, : plan.cells_z] for slot in range(rows, plan.slots)]
    halo += [jnp.zeros_like(halo[0])] * (2 * plan.halo - plan.slots)
    for tile in range(plan.halo):
        even_out[tile], odd_out[tile] = pack(halo[2 * tile], halo[2 * tile + 1], is_even)

    flat = grown[...].reshape(grown.shape[0] * ring, depth)
    high = flat.astype(jnp.bfloat16)
    low = (flat - high.astype(jnp.float32)).astype(jnp.bfloat16)
    product = functools.partial(jnp.dot, preferred_element_type=jnp.float32)

    def chunk(number, carry):
        spread = product(high, z_high[number]) + (
            product(high, z_low[number]) + product(low, z_high[number])
        )
        sums = [jnp.zeros((ring, LANES), jnp.float32) for _ in range(3)]
        for slot in range(plan.slots):
            piece = spread[slot * ring : (slot + 1) * ring]
            for k, part in enumerate((piece[:, :LANES], piece[:, :LANES], piece[:, LANES:])):
                sums[k] += r_fac[number, k, pl.ds(slot, 1), :] * part
        total = [
            jnp.sum(a_fac[number, turn] * sums[k], axis=0, keepdims=True)
            for k, turn in enumerate((0, 1, 0))
        ]
        total.append(jnp.zeros((5, LANES), jnp.float32))
        force_out[number] = jnp.concatenate(total, axis=0)
        return carry

    if plan.chunks == 1:
        chunk(0, 0)
    else:
        lax.fori_loop(0, plan.chunks, chunk, 0)


def join_kernel(plan, even, *refs):
    forces, out = refs[:-1], refs[-1]
    out[: plan.halo] = even[...]
    out[plan.halo :] = forces[0][...] if len(forces) == 1 else forces[0][...] + forces[1][...]


def fold_kernel(plan, edge, even, even_in, odd_in, edge_out, force_out):
    is_even = even_sector(lax.axis_index("ang"))
    for slot in range(plan.beyond):
        tile, half = divmod(plan.cells_r + slot, 2)
        first, last = unpack(even_in[tile], odd_in[tile], half, is_even)
        edge_out[2 * slot] = edge[2 * slot] + first
        edge_out[2 * slot + 1] = edge[2 * slot + 1] + last
    force_out[...] = even[plan.halo :] + even_in[plan.halo :]


def meet_kernel(plan, first, second, *refs):
    half = len(refs) // 2
    refs[half][...] = first[...] + second[...]
    for mid, out in zip(refs[:half], refs[half + 1 :]):
        out[...] = mid[...]


def copy_kernel(plan, value, after, out):
    out[...] = value[...]


def final_kernel(plan, *refs):
    own, mids, edges = refs[0], refs[1 : 1 + plan.sides], refs[1 + plan.sides : 1 + 2 * plan.sides]
    even_in, odd_in, force, out, force_out = refs[-5:]
    force_out[...] = force[...]
    rad = lax.axis_index("rad")
    is_even = even_sector(lax.axis_index("ang"))
    top, inner = plan.cells_a - 8, plan.tiles - 2
    for row in range(plan.cells_r):
        first, last = unpack(even_in[row // 2], odd_in[row // 2], row % 2, is_even)
        out[row] = own[row]
        out[row, 0:8, :] += first
        out[row, top:, :] += last
    for side in range(plan.sides):
        for step in range(1, SWEEPS + 1):
            row = plan.landing_row(side, rad, step)
            out[row, 0:8, :] += edges[side][2 * step - 2]
            out[row, top:, :] += edges[side][2 * step - 1]
            for tile in range(inner):
                out[row, 8 * tile + 8 : 8 * tile + 16, :] += mids[side][(step - 1) * inner + tile]


def call(kernel, plan, outs, scratch, flops, bytes_moved, args, spaces=None, megabytes=24):
    in_vmem = pl.BlockSpec(memory_space=pltpu.VMEM)
    return pl.pallas_call(
        functools.partial(kernel, plan),
        out_shape=[
            out if hasattr(out, "dtype") else jax.ShapeDtypeStruct(out, jnp.float32) for out in outs
        ],
        in_specs=spaces or [in_vmem] * len(args),
        out_specs=[in_vmem] * len(outs),
        scratch_shapes=scratch,
        compiler_params=pltpu.CompilerParams(vmem_limit_bytes=megabytes * 2**20),
        cost_estimate=pl.CostEstimate(flops=flops, bytes_accessed=bytes_moved, transcendentals=0),
    )(*args)


def shards(plan, potential, density, anchor, extent, center, charge, place):
    ring, depth, slots, chunks = plan.ring, plan.total_z, plan.slots, plan.chunks
    rows, width, block = plan.cells_r, plan.cells_z, potential.shape
    swap = [(0, 1), (1, 0)]
    potential_other = lax.ppermute(potential, "ax", swap)
    density_other = lax.ppermute(density, "ax", swap)
    tables = (anchor, extent, center, charge.reshape(1, -1), place.reshape(1, -1))
    tall = rows + 2 * plan.guard
    axial = jax.ShapeDtypeStruct((chunks, depth, 2 * LANES), jnp.bfloat16)
    *factors, coef, potential, density = call(
        factors_kernel,
        plan,
        [axial, axial, (chunks, 2, ring, LANES), (chunks, 3, slots, LANES)]
        + [(4, tall, depth), block, block],
        [pltpu.VMEM(table.shape, table.dtype) for table in tables] + [pltpu.SemaphoreType.DMA((7,))],
        10**6,
        10**6,
        [pltpu.with_memory_space_constraint(value, pltpu.HBM) for value in (*tables, potential, density)],
        [pl.BlockSpec(memory_space=pl.ANY)] * 7,
    )
    (begun,) = call(
        start_kernel,
        plan,
        [(rows + plan.sides, ring, depth)],
        [],
        10**7,
        10**7,
        (potential, potential_other, coef),
    )
    scratch = [(tall, ring, depth)] * 2 + [(2 * plan.halo, ring, depth)]
    inner = SWEEPS * (plan.tiles - 2)
    own, even, odd, mid, edge, force = call(
        sweeps_kernel,
        plan,
        [block, (plan.halo, 8, width), (plan.halo, 8, width)]
        + [(max(1, inner * plan.sides), 8, width), (max(1, 2 * plan.beyond), 8, width)]
        + [(chunks, 8, LANES)],
        [pltpu.VMEM(shape, jnp.float32) for shape in scratch],
        10**9,
        10**7,
        (begun, density, density_other, coef, *factors),
    )

    def send(value, move):
        return lax.ppermute(value, AXES, plan.moves(move))

    def send_radial(value, length):
        if plan.sides == 0:
            return []
        if plan.sides == 1:
            return [send(value, lambda r, a: (1 - r, a))]
        last = plan.n_rad - 1
        return [
            send(value[length : 2 * length], lambda r, a: (r - 1, a) if r else None),
            send(value[:length], lambda r, a: (r + 1, a) if r < last else None),
        ]

    def send_angular(value, step):
        return send(value, lambda r, a: (r, a ^ step))

    (odd,) = call(copy_kernel, plan, [odd.shape], [], 10**6, 10**6, (odd, force))
    odd_in = send(odd, lambda r, a: (r, (a + 1 - 2 * (1 - a % 2)) % plan.n_ang))
    parts = [force]
    step = plan.n_ang // 2
    while step > 2:
        force = sum(parts)
        parts = [force, send_angular(force, step)]
        step //= 2
    (even,) = call(
        join_kernel, plan, [(plan.halo + chunks, 8, width)], [], 10**9, 10**9, (even, *parts)
    )
    even_in = send_angular(even, 1)
    (mid,) = call(copy_kernel, plan, [mid.shape], [], 10**6, 10**6, (mid, even))
    mids = send_radial(mid, inner)
    (odd_in,) = call(copy_kernel, plan, [odd.shape], [], 10**9, 10**9, (odd_in, odd))
    edge, force = call(
        fold_kernel,
        plan,
        [edge.shape, (chunks, 8, LANES)],
        [],
        10**5,
        10**5,
        (edge, even, even_in, odd_in),
    )
    (edge,) = call(copy_kernel, plan, [edge.shape], [], 10**6, 10**6, (edge, force))
    edges = send_radial(edge, 2 * SWEEPS)
    step = 1
    while step < plan.n_rad:
        part = send(force, lambda r, a: (r ^ step, a))
        step *= 2
        if step < plan.n_rad:
            force = force + part
        else:
            shapes = [value.shape for value in (force, *mids)]
            force, *mids = call(meet_kernel, plan, shapes, [], 10**9, 10**9, (force, part, *mids))
    last_part = send_angular(force, 2) if plan.n_ang > 2 else jnp.zeros_like(force)
    final, force = call(
        final_kernel,
        plan,
        [block, force.shape],
        [],
        10**5,
        10**6,
        (own, *mids, *edges, even_in, odd_in, force),
    )
    force = force + last_part
    share = plan.atoms // (plan.n_rad * plan.n_ang * plan.n_ax)
    first = plan.device(*(lax.axis_index(name) for name in AXES)) * share
    mine = lax.dynamic_slice(force, (first // LANES, 0, first % LANES), (1, 3, share))
    return final, mine.reshape(3, share)


def solution(mesh):
    whole = P("rad", "ang", "ax")

    def run(potential, density, anchor, extent, center, charge, place):
        sizes = [mesh.shape[name] for name in AXES]
        block = [total // parts for total, parts in zip(potential.shape, sizes)]
        plan = Plan(mesh, block, charge.shape[0])
        return jax.shard_map(
            functools.partial(shards, plan),
            mesh=mesh,
            in_specs=(whole, whole, P(), P(), P(), P(), P()),
            out_specs=(whole, P(None, AXES)),
            check_vma=False,
        )(potential, density, anchor, extent, center, charge, place)

    return run
```

```python
import functools
import math

import jax
import jax.numpy as jnp
from jax import lax
from jax.experimental import pallas as pl
from jax.experimental.pallas import tpu as pltpu
from jax.sharding import PartitionSpec as P

SWEEPS = 3
LANES = 128
AXES = ("rad", "ang", "ax")

cheb_low = 0.2
cheb_high = 2.0
highest = lax.Precision.HIGHEST


def sweep_weights(total_sweeps):
    middle = 0.5 * (cheb_high + cheb_low)
    spread = 0.5 * (cheb_high - cheb_low)
    return [
        1.0 / (middle + spread * math.cos(math.pi * (2 * number + 1) / (2 * total_sweeps)))
        for number in range(total_sweeps)
    ]


class Plan:
    def __init__(self, mesh, block, atoms):
        self.n_rad, self.n_ang, self.n_ax = (mesh.shape[name] for name in AXES)
        self.cells_r, self.cells_a, self.cells_z = block
        self.atoms = atoms
        self.chunks = atoms // LANES
        self.ring = self.cells_a + 8
        self.total_r = self.cells_r * self.n_rad
        self.total_a = self.cells_a * self.n_ang
        self.total_z = self.cells_z * self.n_ax
        self.angle_step = 2.0 * math.pi / self.total_a
        self.sides = 0 if self.n_rad == 1 else 1 if self.n_rad == 2 else 2
        self.slots = self.cells_r + SWEEPS * self.sides
        self.guard = SWEEPS + 1
        self.beyond = SWEEPS * self.sides
        self.tiles = self.cells_a // 8
        self.halo = (self.slots + 1) // 2

    def sign(self, side, rad):
        if self.sides == 1:
            return 1 - 2 * rad
        return 1 - 2 * side

    def side_row(self, side, rad, step):
        sign = self.sign(side, rad)
        return (self.cells_r - 1) * (1 + sign) // 2 + sign * step

    def landing_row(self, side, rad, step):
        sign = self.sign(side, rad)
        return (self.cells_r - 1) * (1 + sign) // 2 - sign * (step - 1)

    def device(self, rad, ang, ax):
        return (rad * self.n_ang + ang) * self.n_ax + ax

    def moves(self, move):
        found = []
        for rad in range(self.n_rad):
            for ang in range(self.n_ang):
                target = move(rad, ang)
                if target is not None:
                    for ax in range(self.n_ax):
                        found.append((self.device(rad, ang, ax), self.device(*target, 1 - ax)))
        return found


def even_sector(ang):
    return (lax.broadcasted_iota(jnp.int32, (8, LANES), 0) * 0 + ang) % 2 == 0


def pack(front, back, is_even):
    low_half = lax.broadcasted_iota(jnp.int32, front.shape, 0) < 4
    above = jnp.where(low_half, front, pltpu.roll(back, 4, 0))
    below = jnp.where(low_half, pltpu.roll(front, 4, 0), back)
    return jnp.where(is_even, above, below), jnp.where(is_even, below, above)


def unpack(even, odd, half, is_even):
    low_half = lax.broadcasted_iota(jnp.int32, even.shape, 0) < 4
    above, below = jnp.where(is_even, even, odd), jnp.where(is_even, odd, even)
    first = below if half == 0 else pltpu.roll(below, 4, 0)
    last = above if half == 1 else pltpu.roll(above, 4, 0)
    return jnp.where(low_half, first, 0.0), jnp.where(low_half, 0.0, last)


def factors_kernel(plan, *refs):
    sources, outs, held = refs[:7], refs[7:14], refs[14:19]
    z_high, z_low, a_out, r_out, coef, pot_out, rho_out = outs
    copies = [
        pltpu.make_async_copy(source, target, refs[19].at[k])
        for k, (source, target) in enumerate(zip(sources, (*held, pot_out, rho_out)))
    ]
    for copy in copies:
        copy.start()
    rad, ang, ax = (lax.axis_index(name) for name in AXES)
    level = lax.broadcasted_iota(jnp.int32, coef.shape[1:], 0) - plan.guard + rad * plan.cells_r
    valid = (level >= 0) & (level < plan.total_r)
    radius = 0.5 * plan.total_r + level.astype(jnp.float32) + 0.5
    upper, lower = (radius + 0.5) / radius, (radius - 0.5) / radius
    angular = 1.0 / (radius * radius * (plan.angle_step * plan.angle_step))
    diagonal = upper + lower + 2.0 * angular + 2.0
    inverse = jnp.where(valid, 1.0 / diagonal, 0.0)
    coef[0] = upper
    coef[1] = lower
    coef[2] = angular
    coef[3] = inverse

    for copy in copies[:5]:
        copy.wait()
    anchor, extent, center, charge, place = held
    width_r, width_a, width_z = plan.cells_r / 3.0, plan.cells_a / 3.0, plan.cells_z / 3.0
    amplitude = 1.0 / math.sqrt(width_a * width_z / width_r)
    table = jnp.concatenate(
        [
            anchor[...].astype(jnp.float32),
            extent[...].astype(jnp.float32),
            center[...],
            charge[...],
            jnp.zeros((6, plan.atoms), jnp.float32),
        ],
        axis=0,
    )

    def pair(cell, start, span, middle, width, total):
        shifted = cell - start
        if total is not None:
            shifted = jnp.where(shifted < 0.0, shifted + total, shifted)
        distance = shifted + start - middle
        inside = (shifted >= 0.0) & (shifted < span)
        profile = jnp.where(inside, jnp.exp(-(distance * distance) / (2.0 * width * width)), 0.0)
        return profile, profile * (-distance / (width * width))

    def chunk(number, carry):
        rows = lax.broadcasted_iota(jnp.int32, (LANES, plan.atoms), 0) + number * LANES
        onehot = (place[...] == rows).astype(jnp.float32)
        ordered = lax.dot_general(
            table,
            onehot,
            (((1,), (1,)), ((), ())),
            precision=highest,
            preferred_element_type=jnp.float32,
        )
        row = [ordered[k : k + 1, :] for k in range(10)]
        depth = lax.broadcasted_iota(jnp.int32, (plan.total_z, LANES), 0) + ax * plan.cells_z
        depth = jnp.where(depth >= plan.total_z, depth - plan.total_z, depth).astype(jnp.float32)
        profile, slope = pair(
            depth, row[2] * plan.cells_z, row[5] * plan.cells_z, row[8], width_z, plan.total_z
        )
        factor = jnp.concatenate([profile, slope], axis=1)
        high = factor.astype(jnp.bfloat16)
        z_high[number] = high
        z_low[number] = (factor - high.astype(jnp.float32)).astype(jnp.bfloat16)
        spot = lax.broadcasted_iota(jnp.int32, (plan.ring, LANES), 0)
        spot = jnp.where(spot < plan.cells_a + 4, spot, spot - plan.ring) + ang * plan.cells_a
        spot = jnp.where(spot < 0, spot + plan.total_a, spot)
        spot = jnp.where(spot >= plan.total_a, spot - plan.total_a, spot).astype(jnp.float32)
        profile, slope = pair(
            spot, row[1] * plan.cells_a, row[4] * plan.cells_a, row[7], width_a, plan.total_a
        )
        a_out[number, 0] = profile
        a_out[number, 1] = slope
        slot = lax.broadcasted_iota(jnp.int32, (plan.slots, LANES), 0)
        level = slot
        for side in range(plan.sides):
            first = plan.cells_r + SWEEPS * side
            level = jnp.where(slot >= first, plan.side_row(side, rad, slot - first + 1), level)
        level = (level + rad * plan.cells_r).astype(jnp.float32)
        profile, slope = pair(
            level, row[0] * plan.cells_r, row[3] * plan.cells_r, row[6], width_r, None
        )
        radius = 0.5 * plan.total_r + level + 0.5
        strength = row[9] * amplitude
        r_out[number, 0] = strength * (plan.angle_step * radius) * slope
        r_out[number, 1] = strength * profile
        r_out[number, 2] = strength * (plan.angle_step * radius) * profile
        return carry

    if plan.chunks == 1:
        chunk(0, 0)
    else:
        lax.fori_loop(0, plan.chunks, chunk, 0)
    for copy in copies[5:]:
        copy.wait()


def whole(plan, own, other, row):
    blank = jnp.zeros((plan.ring - plan.cells_a, plan.total_z), jnp.float32)
    return jnp.concatenate([jnp.concatenate([own[row], other[row]], axis=1), blank], axis=0)


def around(plan, center, turn):
    total = pltpu.roll(center, 1, 1) + pltpu.roll(center, plan.total_z - 1, 1)
    return total + turn * (pltpu.roll(center, 1, 0) + pltpu.roll(center, plan.ring - 1, 0))


def start_kernel(plan, pot_own, pot_other, coef, out):
    rad = lax.axis_index("rad")
    rows, weight = plan.cells_r, sweep_weights(SWEEPS)[0]
    plane = functools.partial(whole, plan, pot_own, pot_other)
    for row in range(rows):
        up, down, turn, inverse = (coef[k, pl.ds(plan.guard + row, 1), :] for k in range(4))
        center = plane(row)
        total = around(plan, center, turn)
        if row + 1 < rows:
            total += up * plane(row + 1)
        if row > 0:
            total += down * plane(row - 1)
        out[row] = (1.0 - weight) * center + (weight * inverse) * total
    for side in range(plan.sides):
        place = plan.guard + plan.side_row(side, rad, 1)
        up, down, _, inverse = (coef[k, pl.ds(place, 1), :] for k in range(4))
        factor = jnp.where(plan.sign(side, rad) > 0, down, up)
        out[rows + side] = (weight * inverse * factor) * plane(plan.side_row(side, rad, 0))


def sweeps_kernel(
    plan,
    begun,
    rho_own,
    rho_other,
    coef,
    z_high,
    z_low,
    a_fac,
    r_fac,
    own_out,
    even_out,
    odd_out,
    mid_out,
    edge_out,
    force_out,
    first,
    second,
    grown,
):
    rad = lax.axis_index("rad")
    guard, rows, ring, depth = plan.guard, plan.cells_r, plan.ring, plan.total_z
    weights = sweep_weights(SWEEPS)

    blank = jnp.zeros((ring, depth), jnp.float32)
    for buffer in (first, second):
        for row in range(guard):
            buffer[row] = blank
            buffer[guard + rows + row] = blank
    for row in range(rows):
        inverse = coef[3, pl.ds(guard + row, 1), :]
        charge = whole(plan, rho_own, rho_other, row)
        first[guard + row] = begun[row] + (weights[0] * inverse) * charge
    for side in range(plan.sides):
        first[guard + plan.side_row(side, rad, 1)] = begun[rows + side]
    for slot in range(plan.slots, grown.shape[0]):
        grown[slot] = blank

    def relaxed(source, row, weight, charge):
        center = source[row]
        up, down, turn, inverse = (coef[k, pl.ds(row, 1), :] for k in range(4))
        total = around(plan, center, turn)
        total += up * source[row + 1] + down * source[row - 1]
        if charge is not None:
            total += charge
        return (1.0 - weight) * center + (weight * inverse) * total

    def send_row(slot, fresh):
        part = [fresh[8 * tile : 8 * tile + 8, plan.cells_z :] for tile in range(plan.tiles)]
        edge_out[2 * slot], edge_out[2 * slot + 1] = part[0], part[-1]
        for tile in range(1, plan.tiles - 1):
            mid_out[slot * (plan.tiles - 2) + tile - 1] = part[tile]

    source, target = first, second
    for sweep in range(1, SWEEPS):
        last = sweep == SWEEPS - 1
        for row in range(rows):
            fresh = relaxed(source, guard + row, weights[sweep], whole(plan, rho_own, rho_other, row))
            if last:
                grown[row] = fresh
                own_out[row] = fresh[: plan.cells_a, : plan.cells_z]
            else:
                target[guard + row] = fresh
        for side in range(plan.sides):
            for step in range(1, sweep + 2):
                place = guard + plan.side_row(side, rad, step)
                fresh = relaxed(source, place, weights[sweep], None)
                if last:
                    slot = SWEEPS * side + step - 1
                    grown[rows + slot] = fresh
                    send_row(slot, fresh)
                else:
                    target[place] = fresh
        source, target = target, source

    is_even = even_sector(lax.axis_index("ang"))
    halo = [grown[slot, plan.cells_a :, plan.cells_z :] for slot in range(rows)]
    halo += [grown[slot, plan.cells_a :, : plan.cells_z] for slot in range(rows, plan.slots)]
    halo += [jnp.zeros_like(halo[0])] * (2 * plan.halo - plan.slots)
    for tile in range(plan.halo):
        even_out[tile], odd_out[tile] = pack(halo[2 * tile], halo[2 * tile + 1], is_even)

    flat = grown[...].reshape(grown.shape[0] * ring, depth)
    high = flat.astype(jnp.bfloat16)
    low = (flat - high.astype(jnp.float32)).astype(jnp.bfloat16)
    product = functools.partial(jnp.dot, preferred_element_type=jnp.float32)

    def chunk(number, carry):
        spread = product(high, z_high[number]) + (
            product(high, z_low[number]) + product(low, z_high[number])
        )
        sums = [jnp.zeros((ring, LANES), jnp.float32) for _ in range(3)]
        for slot in range(plan.slots):
            piece = spread[slot * ring : (slot + 1) * ring]
            for k, part in enumerate((piece[:, :LANES], piece[:, :LANES], piece[:, LANES:])):
                sums[k] += r_fac[number, k, pl.ds(slot, 1), :] * part
        total = [
            jnp.sum(a_fac[number, turn] * sums[k], axis=0, keepdims=True)
            for k, turn in enumerate((0, 1, 0))
        ]
        total.append(jnp.zeros((5, LANES), jnp.float32))
        force_out[number] = jnp.concatenate(total, axis=0)
        return carry

    if plan.chunks == 1:
        chunk(0, 0)
    else:
        lax.fori_loop(0, plan.chunks, chunk, 0)


def join_kernel(plan, even, *refs):
    forces, out = refs[:-1], refs[-1]
    out[: plan.halo] = even[...]
    out[plan.halo :] = forces[0][...] if len(forces) == 1 else forces[0][...] + forces[1][...]


def sum_kernel(plan, even, even_in, out):
    out[...] = even[plan.halo :] + even_in[plan.halo :]


def fold_kernel(plan, edge, even_in, odd_in, *refs):
    forces, edge_out, force_out = refs[:-2], refs[-2], refs[-1]
    is_even = even_sector(lax.axis_index("ang"))
    for slot in range(plan.beyond):
        tile, half = divmod(plan.cells_r + slot, 2)
        first, last = unpack(even_in[tile], odd_in[tile], half, is_even)
        edge_out[2 * slot] = edge[2 * slot] + first
        edge_out[2 * slot + 1] = edge[2 * slot + 1] + last
    force_out[...] = forces[0][...] if len(forces) == 1 else forces[0][...] + forces[1][...]


def meet_kernel(plan, first, second, *refs):
    half = len(refs) // 2
    refs[half][...] = first[...] + second[...]
    for mid, out in zip(refs[:half], refs[half + 1 :]):
        out[...] = mid[...]


def copy_kernel(plan, value, after, out):
    out[...] = value[...]


def final_kernel(plan, *refs):
    own, mids, edges = refs[0], refs[1 : 1 + plan.sides], refs[1 + plan.sides : 1 + 2 * plan.sides]
    even_in, odd_in, force, out, force_out = refs[-5:]
    force_out[...] = force[...]
    rad = lax.axis_index("rad")
    is_even = even_sector(lax.axis_index("ang"))
    top, inner = plan.cells_a - 8, plan.tiles - 2
    for row in range(plan.cells_r):
        first, last = unpack(even_in[row // 2], odd_in[row // 2], row % 2, is_even)
        out[row] = own[row]
        out[row, 0:8, :] += first
        out[row, top:, :] += last
    for side in range(plan.sides):
        for step in range(1, SWEEPS + 1):
            row = plan.landing_row(side, rad, step)
            out[row, 0:8, :] += edges[side][2 * step - 2]
            out[row, top:, :] += edges[side][2 * step - 1]
            for tile in range(inner):
                out[row, 8 * tile + 8 : 8 * tile + 16, :] += mids[side][(step - 1) * inner + tile]


def call(kernel, plan, outs, scratch, flops, bytes_moved, args, spaces=None, megabytes=24):
    in_vmem = pl.BlockSpec(memory_space=pltpu.VMEM)
    return pl.pallas_call(
        functools.partial(kernel, plan),
        out_shape=[
            out if hasattr(out, "dtype") else jax.ShapeDtypeStruct(out, jnp.float32) for out in outs
        ],
        in_specs=spaces or [in_vmem] * len(args),
        out_specs=[in_vmem] * len(outs),
        scratch_shapes=scratch,
        compiler_params=pltpu.CompilerParams(vmem_limit_bytes=megabytes * 2**20),
        cost_estimate=pl.CostEstimate(flops=flops, bytes_accessed=bytes_moved, transcendentals=0),
    )(*args)


def shards(plan, potential, density, anchor, extent, center, charge, place):
    ring, depth, slots, chunks = plan.ring, plan.total_z, plan.slots, plan.chunks
    rows, width, block = plan.cells_r, plan.cells_z, potential.shape
    swap = [(0, 1), (1, 0)]
    potential_other = lax.ppermute(potential, "ax", swap)
    density_other = lax.ppermute(density, "ax", swap)
    tables = (anchor, extent, center, charge.reshape(1, -1), place.reshape(1, -1))
    tall = rows + 2 * plan.guard
    axial = jax.ShapeDtypeStruct((chunks, depth, 2 * LANES), jnp.bfloat16)
    *factors, coef, potential, density = call(
        factors_kernel,
        plan,
        [axial, axial, (chunks, 2, ring, LANES), (chunks, 3, slots, LANES)]
        + [(4, tall, depth), block, block],
        [pltpu.VMEM(table.shape, table.dtype) for table in tables] + [pltpu.SemaphoreType.DMA((7,))],
        10**6,
        10**6,
        [pltpu.with_memory_space_constraint(value, pltpu.HBM) for value in (*tables, potential, density)],
        [pl.BlockSpec(memory_space=pl.ANY)] * 7,
    )
    (begun,) = call(
        start_kernel,
        plan,
        [(rows + plan.sides, ring, depth)],
        [],
        10**7,
        10**7,
        (potential, potential_other, coef),
    )
    scratch = [(tall, ring, depth)] * 2 + [(2 * plan.halo, ring, depth)]
    inner = SWEEPS * (plan.tiles - 2)
    own, even, odd, mid, edge, force = call(
        sweeps_kernel,
        plan,
        [block, (plan.halo, 8, width), (plan.halo, 8, width)]
        + [(max(1, inner * plan.sides), 8, width), (max(1, 2 * plan.beyond), 8, width)]
        + [(chunks, 8, LANES)],
        [pltpu.VMEM(shape, jnp.float32) for shape in scratch],
        10**9,
        10**7,
        (begun, density, density_other, coef, *factors),
    )

    def send(value, move):
        return lax.ppermute(value, AXES, plan.moves(move))

    def send_radial(value, length):
        if plan.sides == 0:
            return []
        if plan.sides == 1:
            return [send(value, lambda r, a: (1 - r, a))]
        last = plan.n_rad - 1
        return [
            send(value[length : 2 * length], lambda r, a: (r - 1, a) if r else None),
            send(value[:length], lambda r, a: (r + 1, a) if r < last else None),
        ]

    def send_angular(value, step):
        return send(value, lambda r, a: (r, a ^ step))

    (even,) = call(
        join_kernel, plan, [(plan.halo + chunks, 8, width)], [], 10**5, 10**5, (even, force)
    )
    even_in = send_angular(even, 1)
    (odd,) = call(copy_kernel, plan, [odd.shape], [], 10**6, 10**6, (odd, even))
    odd_in = send(odd, lambda r, a: (r, (a + 1 - 2 * (1 - a % 2)) % plan.n_ang))
    (force,) = call(sum_kernel, plan, [force.shape], [], 10**9, 10**9, (even, even_in))
    (mid,) = call(copy_kernel, plan, [mid.shape], [], 10**6, 10**6, (mid, force))
    mids = send_radial(mid, inner)
    parts = [force]
    step = plan.n_ang // 2
    while step > 2:
        force = sum(parts)
        parts = [force, send_angular(force, step)]
        step //= 2
    (odd_in,) = call(copy_kernel, plan, [odd.shape], [], 10**9, 10**9, (odd_in, odd))
    edge, force = call(
        fold_kernel,
        plan,
        [edge.shape, (chunks, 8, LANES)],
        [],
        10**5,
        10**5,
        (edge, even_in, odd_in, *parts),
    )
    (edge,) = call(copy_kernel, plan, [edge.shape], [], 10**6, 10**6, (edge, force))
    edges = send_radial(edge, 2 * SWEEPS)
    step = 1
    while step < plan.n_rad:
        part = send(force, lambda r, a: (r ^ step, a))
        step *= 2
        if step < plan.n_rad:
            force = force + part
        else:
            shapes = [value.shape for value in (force, *mids)]
            force, *mids = call(meet_kernel, plan, shapes, [], 10**9, 10**9, (force, part, *mids))
    last_part = send_angular(force, 2) if plan.n_ang > 2 else jnp.zeros_like(force)
    final, force = call(
        final_kernel,
        plan,
        [block, force.shape],
        [],
        10**5,
        10**6,
        (own, *mids, *edges, even_in, odd_in, force),
    )
    force = force + last_part
    share = plan.atoms // (plan.n_rad * plan.n_ang * plan.n_ax)
    first = plan.device(*(lax.axis_index(name) for name in AXES)) * share
    mine = lax.dynamic_slice(force, (first // LANES, 0, first % LANES), (1, 3, share))
    return final, mine.reshape(3, share)


def solution(mesh):
    whole = P("rad", "ang", "ax")

    def run(potential, density, anchor, extent, center, charge, place):
        sizes = [mesh.shape[name] for name in AXES]
        block = [total // parts for total, parts in zip(potential.shape, sizes)]
        plan = Plan(mesh, block, charge.shape[0])
        return jax.shard_map(
            functools.partial(shards, plan),
            mesh=mesh,
            in_specs=(whole, whole, P(), P(), P(), P(), P()),
            out_specs=(whole, P(None, AXES)),
            check_vma=False,
        )(potential, density, anchor, extent, center, charge, place)

    return run
```

```python
import functools
import math

import jax
import jax.numpy as jnp
from jax import lax
from jax.experimental import pallas as pl
from jax.experimental.pallas import tpu as pltpu
from jax.sharding import PartitionSpec as P

SWEEPS = 3
LANES = 128
AXES = ("rad", "ang", "ax")

cheb_low = 0.2
cheb_high = 2.0
highest = lax.Precision.HIGHEST


def sweep_weights(total_sweeps):
    middle = 0.5 * (cheb_high + cheb_low)
    spread = 0.5 * (cheb_high - cheb_low)
    return [
        1.0 / (middle + spread * math.cos(math.pi * (2 * number + 1) / (2 * total_sweeps)))
        for number in range(total_sweeps)
    ]


class Plan:
    def __init__(self, mesh, block, atoms):
        self.n_rad, self.n_ang, self.n_ax = (mesh.shape[name] for name in AXES)
        self.cells_r, self.cells_a, self.cells_z = block
        self.atoms = atoms
        self.chunks = atoms // LANES
        self.ring = self.cells_a + 8
        self.total_r = self.cells_r * self.n_rad
        self.total_a = self.cells_a * self.n_ang
        self.total_z = self.cells_z * self.n_ax
        self.angle_step = 2.0 * math.pi / self.total_a
        self.sides = 0 if self.n_rad == 1 else 1 if self.n_rad == 2 else 2
        self.slots = self.cells_r + SWEEPS * self.sides
        self.guard = SWEEPS + 1
        self.beyond = SWEEPS * self.sides
        self.tiles = self.cells_a // 8
        self.halo = (self.slots + 1) // 2
        self.pairs = self.cells_r // 2
        self.corners = self.halo - self.pairs

    def sign(self, side, rad):
        if self.sides == 1:
            return 1 - 2 * rad
        return 1 - 2 * side

    def side_row(self, side, rad, step):
        sign = self.sign(side, rad)
        return (self.cells_r - 1) * (1 + sign) // 2 + sign * step

    def landing_row(self, side, rad, step):
        sign = self.sign(side, rad)
        return (self.cells_r - 1) * (1 + sign) // 2 - sign * (step - 1)

    def device(self, rad, ang, ax):
        return (rad * self.n_ang + ang) * self.n_ax + ax

    def moves(self, move):
        found = []
        for rad in range(self.n_rad):
            for ang in range(self.n_ang):
                target = move(rad, ang)
                if target is not None:
                    for ax in range(self.n_ax):
                        found.append((self.device(rad, ang, ax), self.device(*target, 1 - ax)))
        return found


def even_sector(ang):
    return (lax.broadcasted_iota(jnp.int32, (8, LANES), 0) * 0 + ang) % 2 == 0


def pack(front, back, is_even):
    low_half = lax.broadcasted_iota(jnp.int32, front.shape, 0) < 4
    above = jnp.where(low_half, front, pltpu.roll(back, 4, 0))
    below = jnp.where(low_half, pltpu.roll(front, 4, 0), back)
    return jnp.where(is_even, above, below), jnp.where(is_even, below, above)


def unpack(even, odd, half, is_even):
    low_half = lax.broadcasted_iota(jnp.int32, even.shape, 0) < 4
    above, below = jnp.where(is_even, even, odd), jnp.where(is_even, odd, even)
    first = below if half == 0 else pltpu.roll(below, 4, 0)
    last = above if half == 1 else pltpu.roll(above, 4, 0)
    return jnp.where(low_half, first, 0.0), jnp.where(low_half, 0.0, last)


def factors_kernel(plan, *refs):
    sources, outs, held = refs[:7], refs[7:14], refs[14:19]
    z_high, z_low, a_out, r_out, coef, pot_out, rho_out = outs
    copies = [
        pltpu.make_async_copy(source, target, refs[19].at[k])
        for k, (source, target) in enumerate(zip(sources, (*held, pot_out, rho_out)))
    ]
    for copy in copies:
        copy.start()
    rad, ang, ax = (lax.axis_index(name) for name in AXES)
    level = lax.broadcasted_iota(jnp.int32, coef.shape[1:], 0) - plan.guard + rad * plan.cells_r
    valid = (level >= 0) & (level < plan.total_r)
    radius = 0.5 * plan.total_r + level.astype(jnp.float32) + 0.5
    upper, lower = (radius + 0.5) / radius, (radius - 0.5) / radius
    angular = 1.0 / (radius * radius * (plan.angle_step * plan.angle_step))
    diagonal = upper + lower + 2.0 * angular + 2.0
    inverse = jnp.where(valid, 1.0 / diagonal, 0.0)
    coef[0] = upper
    coef[1] = lower
    coef[2] = angular
    coef[3] = inverse

    for copy in copies[:5]:
        copy.wait()
    anchor, extent, center, charge, place = held
    width_r, width_a, width_z = plan.cells_r / 3.0, plan.cells_a / 3.0, plan.cells_z / 3.0
    amplitude = 1.0 / math.sqrt(width_a * width_z / width_r)
    table = jnp.concatenate(
        [
            anchor[...].astype(jnp.float32),
            extent[...].astype(jnp.float32),
            center[...],
            charge[...],
            jnp.zeros((6, plan.atoms), jnp.float32),
        ],
        axis=0,
    )

    def pair(cell, start, span, middle, width, total):
        shifted = cell - start
        if total is not None:
            shifted = jnp.where(shifted < 0.0, shifted + total, shifted)
        distance = shifted + start - middle
        inside = (shifted >= 0.0) & (shifted < span)
        profile = jnp.where(inside, jnp.exp(-(distance * distance) / (2.0 * width * width)), 0.0)
        return profile, profile * (-distance / (width * width))

    def chunk(number, carry):
        rows = lax.broadcasted_iota(jnp.int32, (LANES, plan.atoms), 0) + number * LANES
        onehot = (place[...] == rows).astype(jnp.float32)
        ordered = lax.dot_general(
            table,
            onehot,
            (((1,), (1,)), ((), ())),
            precision=highest,
            preferred_element_type=jnp.float32,
        )
        row = [ordered[k : k + 1, :] for k in range(10)]
        depth = lax.broadcasted_iota(jnp.int32, (plan.total_z, LANES), 0) + ax * plan.cells_z
        depth = jnp.where(depth >= plan.total_z, depth - plan.total_z, depth).astype(jnp.float32)
        profile, slope = pair(
            depth, row[2] * plan.cells_z, row[5] * plan.cells_z, row[8], width_z, plan.total_z
        )
        factor = jnp.concatenate([profile, slope], axis=1)
        high = factor.astype(jnp.bfloat16)
        z_high[number] = high
        z_low[number] = (factor - high.astype(jnp.float32)).astype(jnp.bfloat16)
        spot = lax.broadcasted_iota(jnp.int32, (plan.ring, LANES), 0)
        spot = jnp.where(spot < plan.cells_a + 4, spot, spot - plan.ring) + ang * plan.cells_a
        spot = jnp.where(spot < 0, spot + plan.total_a, spot)
        spot = jnp.where(spot >= plan.total_a, spot - plan.total_a, spot).astype(jnp.float32)
        profile, slope = pair(
            spot, row[1] * plan.cells_a, row[4] * plan.cells_a, row[7], width_a, plan.total_a
        )
        a_out[number, 0] = profile
        a_out[number, 1] = slope
        slot = lax.broadcasted_iota(jnp.int32, (plan.slots, LANES), 0)
        level = slot
        for side in range(plan.sides):
            first = plan.cells_r + SWEEPS * side
            level = jnp.where(slot >= first, plan.side_row(side, rad, slot - first + 1), level)
        level = (level + rad * plan.cells_r).astype(jnp.float32)
        profile, slope = pair(
            level, row[0] * plan.cells_r, row[3] * plan.cells_r, row[6], width_r, None
        )
        radius = 0.5 * plan.total_r + level + 0.5
        strength = row[9] * amplitude
        r_out[number, 0] = strength * (plan.angle_step * radius) * slope
        r_out[number, 1] = strength * profile
        r_out[number, 2] = strength * (plan.angle_step * radius) * profile
        return carry

    if plan.chunks == 1:
        chunk(0, 0)
    else:
        lax.fori_loop(0, plan.chunks, chunk, 0)
    for copy in copies[5:]:
        copy.wait()


def whole(plan, own, other, row):
    blank = jnp.zeros((plan.ring - plan.cells_a, plan.total_z), jnp.float32)
    return jnp.concatenate([jnp.concatenate([own[row], other[row]], axis=1), blank], axis=0)


def around(plan, center, turn):
    total = pltpu.roll(center, 1, 1) + pltpu.roll(center, plan.total_z - 1, 1)
    return total + turn * (pltpu.roll(center, 1, 0) + pltpu.roll(center, plan.ring - 1, 0))


def start_kernel(plan, pot_own, pot_other, coef, out):
    rad = lax.axis_index("rad")
    rows, weight = plan.cells_r, sweep_weights(SWEEPS)[0]
    plane = functools.partial(whole, plan, pot_own, pot_other)
    for row in range(rows):
        up, down, turn, inverse = (coef[k, pl.ds(plan.guard + row, 1), :] for k in range(4))
        center = plane(row)
        total = around(plan, center, turn)
        if row + 1 < rows:
            total += up * plane(row + 1)
        if row > 0:
            total += down * plane(row - 1)
        out[row] = (1.0 - weight) * center + (weight * inverse) * total
    for side in range(plan.sides):
        place = plan.guard + plan.side_row(side, rad, 1)
        up, down, _, inverse = (coef[k, pl.ds(place, 1), :] for k in range(4))
        factor = jnp.where(plan.sign(side, rad) > 0, down, up)
        out[rows + side] = (weight * inverse * factor) * plane(plan.side_row(side, rad, 0))


def sweeps_kernel(
    plan,
    begun,
    rho_own,
    rho_other,
    coef,
    z_high,
    z_low,
    a_fac,
    r_fac,
    grown,
    force_out,
    first,
    second,
):
    rad = lax.axis_index("rad")
    guard, rows, ring, depth = plan.guard, plan.cells_r, plan.ring, plan.total_z
    weights = sweep_weights(SWEEPS)

    blank = jnp.zeros((ring, depth), jnp.float32)
    for away in range(1, guard + 1):
        for row in (guard - away, guard + rows - 1 + away):
            if away < guard:
                first[row] = blank
            if away != 2:
                second[row] = blank
    for row in range(rows):
        inverse = coef[3, pl.ds(guard + row, 1), :]
        charge = whole(plan, rho_own, rho_other, row)
        first[guard + row] = begun[row] + (weights[0] * inverse) * charge
    for side in range(plan.sides):
        first[guard + plan.side_row(side, rad, 1)] = begun[rows + side]
    for slot in range(plan.slots, grown.shape[0]):
        grown[slot] = blank

    def relaxed(source, row, weight, charge):
        center = source[row]
        up, down, turn, inverse = (coef[k, pl.ds(row, 1), :] for k in range(4))
        total = around(plan, center, turn)
        total += up * source[row + 1] + down * source[row - 1]
        if charge is not None:
            total += charge
        return (1.0 - weight) * center + (weight * inverse) * total

    source, target = first, second
    for sweep in range(1, SWEEPS):
        last = sweep == SWEEPS - 1
        for row in range(rows):
            fresh = relaxed(source, guard + row, weights[sweep], whole(plan, rho_own, rho_other, row))
            if last:
                grown[row] = fresh
            else:
                target[guard + row] = fresh
        for side in range(plan.sides):
            for step in range(1, sweep + 2):
                place = guard + plan.side_row(side, rad, step)
                fresh = relaxed(source, place, weights[sweep], None)
                if last:
                    slot = SWEEPS * side + step - 1
                    grown[rows + slot] = fresh
                else:
                    target[place] = fresh
        source, target = target, source

    flat = grown[...].reshape(grown.shape[0] * ring, depth)
    high = flat.astype(jnp.bfloat16)
    low = (flat - high.astype(jnp.float32)).astype(jnp.bfloat16)
    product = functools.partial(jnp.dot, preferred_element_type=jnp.float32)

    def chunk(number, carry):
        spread = product(high, z_high[number]) + (
            product(high, z_low[number]) + product(low, z_high[number])
        )
        sums = [jnp.zeros((ring, LANES), jnp.float32) for _ in range(3)]
        for slot in range(plan.slots):
            piece = spread[slot * ring : (slot + 1) * ring]
            for k, part in enumerate((piece[:, :LANES], piece[:, :LANES], piece[:, LANES:])):
                sums[k] += r_fac[number, k, pl.ds(slot, 1), :] * part
        total = [
            jnp.sum(a_fac[number, turn] * sums[k], axis=0, keepdims=True)
            for k, turn in enumerate((0, 1, 0))
        ]
        total.append(jnp.zeros((5, LANES), jnp.float32))
        force_out[number] = jnp.concatenate(total, axis=0)
        return carry

    if plan.chunks == 1:
        chunk(0, 0)
    else:
        lax.fori_loop(0, plan.chunks, chunk, 0)


def halo_tile(plan, grown, tile, is_even):
    planes = []
    for slot in (2 * tile, 2 * tile + 1):
        half = slice(plan.cells_z, None) if slot < plan.cells_r else slice(plan.cells_z)
        planes.append(grown[slot, plan.cells_a :, half])
    return pack(*planes, is_even)


def join_kernel(plan, grown, force, out):
    is_even = even_sector(lax.axis_index("ang"))
    for tile in range(plan.corners):
        out[tile] = halo_tile(plan, grown, plan.pairs + tile, is_even)[0]
    out[plan.corners :] = force[...]


def main_kernel(plan, grown, after, out):
    is_even = even_sector(lax.axis_index("ang"))
    for tile in range(plan.pairs):
        out[tile] = halo_tile(plan, grown, tile, is_even)[0]


def odd_kernel(plan, grown, after, out):
    is_even = even_sector(lax.axis_index("ang"))
    for tile in range(plan.halo):
        out[tile] = halo_tile(plan, grown, tile, is_even)[1]


def mid_kernel(plan, grown, after, out):
    inner = plan.tiles - 2
    for slot in range(plan.beyond):
        for tile in range(inner):
            first = 8 * (tile + 1)
            out[slot * inner + tile] = grown[plan.cells_r + slot, first : first + 8, plan.cells_z :]


def sum_kernel(plan, even, even_in, out):
    out[...] = even[plan.corners :] + even_in[plan.corners :]


def fold_kernel(plan, grown, even_in, odd_in, *refs):
    forces, edge_out, force_out = refs[:-2], refs[-2], refs[-1]
    is_even = even_sector(lax.axis_index("ang"))
    for slot in range(plan.beyond):
        tile, half = divmod(plan.cells_r + slot, 2)
        first, last = unpack(even_in[tile - plan.pairs], odd_in[tile], half, is_even)
        plane, top = plan.cells_r + slot, plan.cells_a - 8
        edge_out[2 * slot] = grown[plane, :8, plan.cells_z :] + first
        edge_out[2 * slot + 1] = grown[plane, top : plan.cells_a, plan.cells_z :] + last
    force_out[...] = forces[0][...] if len(forces) == 1 else forces[0][...] + forces[1][...]


def meet_kernel(plan, first, second, *refs):
    half = len(refs) // 2
    refs[half][...] = first[...] + second[...]
    for mid, out in zip(refs[:half], refs[half + 1 :]):
        out[...] = mid[...]


def copy_kernel(plan, value, after, out):
    out[...] = value[...]


def final_kernel(plan, *refs):
    own, mids, edges = refs[0], refs[1 : 1 + plan.sides], refs[1 + plan.sides : 1 + 2 * plan.sides]
    even_in, odd_in, force, out, force_out = refs[-5:]
    force_out[...] = force[...]
    rad = lax.axis_index("rad")
    is_even = even_sector(lax.axis_index("ang"))
    top, inner = plan.cells_a - 8, plan.tiles - 2
    for row in range(plan.cells_r):
        first, last = unpack(even_in[row // 2], odd_in[row // 2], row % 2, is_even)
        out[row] = own[row, : plan.cells_a, : plan.cells_z]
        out[row, 0:8, :] += first
        out[row, top:, :] += last
    for side in range(plan.sides):
        for step in range(1, SWEEPS + 1):
            row = plan.landing_row(side, rad, step)
            out[row, 0:8, :] += edges[side][2 * step - 2]
            out[row, top:, :] += edges[side][2 * step - 1]
            for tile in range(inner):
                out[row, 8 * tile + 8 : 8 * tile + 16, :] += mids[side][(step - 1) * inner + tile]


def share_kernel(plan, force, part, out):
    share = out.shape[1]
    start = plan.device(*(lax.axis_index(name) for name in AXES)) * share
    total = force[start // LANES] + part[start // LANES]
    turned = pltpu.roll(total, lax.rem(LANES - lax.rem(start, LANES), LANES), 1)
    out[...] = turned[:3, :share]


def call(kernel, plan, outs, scratch, flops, bytes_moved, args, spaces=None, megabytes=24):
    in_vmem = pl.BlockSpec(memory_space=pltpu.VMEM)
    return pl.pallas_call(
        functools.partial(kernel, plan),
        out_shape=[
            out if hasattr(out, "dtype") else jax.ShapeDtypeStruct(out, jnp.float32) for out in outs
        ],
        in_specs=spaces or [in_vmem] * len(args),
        out_specs=[in_vmem] * len(outs),
        scratch_shapes=scratch,
        compiler_params=pltpu.CompilerParams(vmem_limit_bytes=megabytes * 2**20),
        cost_estimate=pl.CostEstimate(flops=flops, bytes_accessed=bytes_moved, transcendentals=0),
    )(*args)


def shards(plan, potential, density, anchor, extent, center, charge, place):
    ring, depth, slots, chunks = plan.ring, plan.total_z, plan.slots, plan.chunks
    rows, width, block = plan.cells_r, plan.cells_z, potential.shape
    swap = [(0, 1), (1, 0)]
    potential_other = lax.ppermute(potential, "ax", swap)
    density_other = lax.ppermute(density, "ax", swap)
    tables = (anchor, extent, center, charge.reshape(1, -1), place.reshape(1, -1))
    tall = rows + 2 * plan.guard
    axial = jax.ShapeDtypeStruct((chunks, depth, 2 * LANES), jnp.bfloat16)
    *factors, coef, potential, density = call(
        factors_kernel,
        plan,
        [axial, axial, (chunks, 2, ring, LANES), (chunks, 3, slots, LANES)]
        + [(4, tall, depth), block, block],
        [pltpu.VMEM(table.shape, table.dtype) for table in tables] + [pltpu.SemaphoreType.DMA((7,))],
        10**6,
        10**6,
        [pltpu.with_memory_space_constraint(value, pltpu.HBM) for value in (*tables, potential, density)],
        [pl.BlockSpec(memory_space=pl.ANY)] * 7,
    )
    (begun,) = call(
        start_kernel,
        plan,
        [(rows + plan.sides, ring, depth)],
        [],
        10**7,
        10**7,
        (potential, potential_other, coef),
    )
    scratch = [(tall, ring, depth)] * 2
    inner = SWEEPS * (plan.tiles - 2)
    grown, force = call(
        sweeps_kernel,
        plan,
        [(2 * plan.halo, ring, depth), (chunks, 8, LANES)],
        [pltpu.VMEM(shape, jnp.float32) for shape in scratch],
        10**9,
        10**7,
        (begun, density, density_other, coef, *factors),
    )

    def send(value, move):
        return lax.ppermute(value, AXES, plan.moves(move))

    def send_radial(value, length):
        if plan.sides == 0:
            return []
        if plan.sides == 1:
            return [send(value, lambda r, a: (1 - r, a))]
        last = plan.n_rad - 1
        return [
            send(value[length : 2 * length], lambda r, a: (r - 1, a) if r else None),
            send(value[:length], lambda r, a: (r + 1, a) if r < last else None),
        ]

    def send_angular(value, step):
        return send(value, lambda r, a: (r, a ^ step))

    (join,) = call(
        join_kernel, plan, [(plan.corners + chunks, 8, width)], [], 10**5, 10**5, (grown, force)
    )
    join_in = send_angular(join, 1)
    odd_shape = (plan.halo, 8, width)
    (odd,) = call(odd_kernel, plan, [odd_shape], [], 10**6, 10**6, (grown, join))
    odd_in = send(odd, lambda r, a: (r, (a + 1 - 2 * (1 - a % 2)) % plan.n_ang))
    (force,) = call(sum_kernel, plan, [force.shape], [], 10**9, 10**9, (join, join_in))
    mid_shape = (max(1, inner * plan.sides), 8, width)
    (mid,) = call(mid_kernel, plan, [mid_shape], [], 10**6, 10**6, (grown, force))
    (even,) = call(
        main_kernel, plan, [(plan.pairs, 8, width)], [], 10**6, 10**6, (grown, force)
    )
    mids = send_radial(mid, inner) + [send_angular(even, 1)]
    parts = [force]
    step = plan.n_ang // 2
    while step > 2:
        force = sum(parts)
        parts = [force, send_angular(force, step)]
        step //= 2
    (odd_in,) = call(copy_kernel, plan, [odd.shape], [], 10**9, 10**9, (odd_in, odd))
    edge, force = call(
        fold_kernel,
        plan,
        [(max(1, 2 * plan.beyond), 8, width), (chunks, 8, LANES)],
        [],
        10**5,
        10**5,
        (grown, join_in, odd_in, *parts),
    )
    (edge,) = call(copy_kernel, plan, [edge.shape], [], 10**6, 10**6, (edge, force))
    edges = send_radial(edge, 2 * SWEEPS)
    step = 1
    while step < plan.n_rad:
        part = send(force, lambda r, a: (r ^ step, a))
        step *= 2
        if step < plan.n_rad:
            force = force + part
        else:
            shapes = [value.shape for value in (force, *mids)]
            force, *mids = call(meet_kernel, plan, shapes, [], 10**9, 10**9, (force, part, *mids))
    *mids, even_in = mids
    last_part = send_angular(force, 2) if plan.n_ang > 2 else jnp.zeros_like(force)
    final, force = call(
        final_kernel,
        plan,
        [block, force.shape],
        [],
        10**5,
        10**6,
        (grown, *mids, *edges, even_in, odd_in, force),
    )
    share = plan.atoms // (plan.n_rad * plan.n_ang * plan.n_ax)
    (mine,) = call(share_kernel, plan, [(3, share)], [], 10**5, 10**5, (force, last_part))
    return final, mine


def solution(mesh):
    whole = P("rad", "ang", "ax")

    def run(potential, density, anchor, extent, center, charge, place):
        sizes = [mesh.shape[name] for name in AXES]
        block = [total // parts for total, parts in zip(potential.shape, sizes)]
        plan = Plan(mesh, block, charge.shape[0])
        return jax.shard_map(
            functools.partial(shards, plan),
            mesh=mesh,
            in_specs=(whole, whole, P(), P(), P(), P(), P()),
            out_specs=(whole, P(None, AXES)),
            check_vma=False,
        )(potential, density, anchor, extent, center, charge, place)

    return run
```

```python
import functools
import math

import jax
import jax.numpy as jnp
from jax import lax
from jax.experimental import pallas as pl
from jax.experimental.pallas import tpu as pltpu
from jax.sharding import PartitionSpec as P

SWEEPS = 3
LANES = 128
GROUP = 4
AXES = ("rad", "ang", "ax")

cheb_low = 0.2
cheb_high = 2.0
highest = lax.Precision.HIGHEST


def sweep_weights(total_sweeps):
    middle = 0.5 * (cheb_high + cheb_low)
    spread = 0.5 * (cheb_high - cheb_low)
    return [
        1.0 / (middle + spread * math.cos(math.pi * (2 * number + 1) / (2 * total_sweeps)))
        for number in range(total_sweeps)
    ]


class Plan:
    def __init__(self, mesh, block, atoms):
        self.n_rad, self.n_ang, self.n_ax = (mesh.shape[name] for name in AXES)
        self.cells_r, self.cells_a, self.cells_z = block
        self.atoms = atoms
        self.chunks = atoms // LANES
        self.ring = self.cells_a + 8
        self.total_r = self.cells_r * self.n_rad
        self.total_a = self.cells_a * self.n_ang
        self.total_z = self.cells_z * self.n_ax
        self.angle_step = 2.0 * math.pi / self.total_a
        self.sides = 0 if self.n_rad == 1 else 1 if self.n_rad == 2 else 2
        self.slots = self.cells_r + SWEEPS * self.sides
        self.guard = SWEEPS + 1
        self.beyond = SWEEPS * self.sides
        self.tiles = self.cells_a // 8
        self.halo = (self.slots + 1) // 2
        self.planes = -(-self.slots // GROUP) * GROUP
        self.pairs = self.cells_r // 2
        self.corners = self.halo - self.pairs

    def sign(self, side, rad):
        if self.sides == 1:
            return 1 - 2 * rad
        return 1 - 2 * side

    def side_row(self, side, rad, step):
        sign = self.sign(side, rad)
        return (self.cells_r - 1) * (1 + sign) // 2 + sign * step

    def landing_row(self, side, rad, step):
        sign = self.sign(side, rad)
        return (self.cells_r - 1) * (1 + sign) // 2 - sign * (step - 1)

    def device(self, rad, ang, ax):
        return (rad * self.n_ang + ang) * self.n_ax + ax

    def moves(self, move):
        found = []
        for rad in range(self.n_rad):
            for ang in range(self.n_ang):
                target = move(rad, ang)
                if target is not None:
                    for ax in range(self.n_ax):
                        found.append((self.device(rad, ang, ax), self.device(*target, 1 - ax)))
        return found


def even_sector(ang):
    return (lax.broadcasted_iota(jnp.int32, (8, LANES), 0) * 0 + ang) % 2 == 0


def pack(front, back, is_even):
    low_half = lax.broadcasted_iota(jnp.int32, front.shape, 0) < 4
    above = jnp.where(low_half, front, pltpu.roll(back, 4, 0))
    below = jnp.where(low_half, pltpu.roll(front, 4, 0), back)
    return jnp.where(is_even, above, below), jnp.where(is_even, below, above)


def unpack(even, odd, half, is_even):
    low_half = lax.broadcasted_iota(jnp.int32, even.shape, 0) < 4
    above, below = jnp.where(is_even, even, odd), jnp.where(is_even, odd, even)
    first = below if half == 0 else pltpu.roll(below, 4, 0)
    last = above if half == 1 else pltpu.roll(above, 4, 0)
    return jnp.where(low_half, first, 0.0), jnp.where(low_half, 0.0, last)


def factors_kernel(plan, *refs):
    sources, outs, held = refs[:7], refs[7:14], refs[14:19]
    z_high, z_low, a_out, r_out, coef, pot_out, rho_out = outs
    copies = [
        pltpu.make_async_copy(source, target, refs[19].at[k])
        for k, (source, target) in enumerate(zip(sources, (*held, pot_out, rho_out)))
    ]
    for copy in copies:
        copy.start()
    rad, ang, ax = (lax.axis_index(name) for name in AXES)
    level = lax.broadcasted_iota(jnp.int32, coef.shape[1:], 0) - plan.guard + rad * plan.cells_r
    valid = (level >= 0) & (level < plan.total_r)
    radius = 0.5 * plan.total_r + level.astype(jnp.float32) + 0.5
    upper, lower = (radius + 0.5) / radius, (radius - 0.5) / radius
    angular = 1.0 / (radius * radius * (plan.angle_step * plan.angle_step))
    diagonal = upper + lower + 2.0 * angular + 2.0
    inverse = jnp.where(valid, 1.0 / diagonal, 0.0)
    coef[0] = upper
    coef[1] = lower
    coef[2] = angular
    coef[3] = inverse

    for copy in copies[:5]:
        copy.wait()
    anchor, extent, center, charge, place = held
    width_r, width_a, width_z = plan.cells_r / 3.0, plan.cells_a / 3.0, plan.cells_z / 3.0
    amplitude = 1.0 / math.sqrt(width_a * width_z / width_r)
    table = jnp.concatenate(
        [
            anchor[...].astype(jnp.float32),
            extent[...].astype(jnp.float32),
            center[...],
            charge[...],
            jnp.zeros((6, plan.atoms), jnp.float32),
        ],
        axis=0,
    )

    def pair(cell, start, span, middle, width, total):
        shifted = cell - start
        if total is not None:
            shifted = jnp.where(shifted < 0.0, shifted + total, shifted)
        distance = shifted + start - middle
        inside = (shifted >= 0.0) & (shifted < span)
        profile = jnp.where(inside, jnp.exp(-(distance * distance) / (2.0 * width * width)), 0.0)
        return profile, profile * (-distance / (width * width))

    def chunk(number, carry):
        rows = lax.broadcasted_iota(jnp.int32, (LANES, plan.atoms), 0) + number * LANES
        onehot = (place[...] == rows).astype(jnp.float32)
        ordered = lax.dot_general(
            table,
            onehot,
            (((1,), (1,)), ((), ())),
            precision=highest,
            preferred_element_type=jnp.float32,
        )
        row = [ordered[k : k + 1, :] for k in range(10)]
        depth = lax.broadcasted_iota(jnp.int32, (plan.total_z, LANES), 0) + ax * plan.cells_z
        depth = jnp.where(depth >= plan.total_z, depth - plan.total_z, depth).astype(jnp.float32)
        profile, slope = pair(
            depth, row[2] * plan.cells_z, row[5] * plan.cells_z, row[8], width_z, plan.total_z
        )
        factor = jnp.concatenate([profile, slope], axis=1)
        high = factor.astype(jnp.bfloat16)
        z_high[number] = high
        z_low[number] = (factor - high.astype(jnp.float32)).astype(jnp.bfloat16)
        spot = lax.broadcasted_iota(jnp.int32, (plan.ring, LANES), 0)
        spot = jnp.where(spot < plan.cells_a + 4, spot, spot - plan.ring) + ang * plan.cells_a
        spot = jnp.where(spot < 0, spot + plan.total_a, spot)
        spot = jnp.where(spot >= plan.total_a, spot - plan.total_a, spot).astype(jnp.float32)
        profile, slope = pair(
            spot, row[1] * plan.cells_a, row[4] * plan.cells_a, row[7], width_a, plan.total_a
        )
        a_out[number, 0] = profile
        a_out[number, 1] = slope
        slot = lax.broadcasted_iota(jnp.int32, (plan.slots, LANES), 0)
        level = slot
        for side in range(plan.sides):
            first = plan.cells_r + SWEEPS * side
            level = jnp.where(slot >= first, plan.side_row(side, rad, slot - first + 1), level)
        level = (level + rad * plan.cells_r).astype(jnp.float32)
        profile, slope = pair(
            level, row[0] * plan.cells_r, row[3] * plan.cells_r, row[6], width_r, None
        )
        radius = 0.5 * plan.total_r + level + 0.5
        strength = row[9] * amplitude
        r_out[number, 0] = strength * (plan.angle_step * radius) * slope
        r_out[number, 1] = strength * profile
        r_out[number, 2] = strength * (plan.angle_step * radius) * profile
        return carry

    if plan.chunks == 1:
        chunk(0, 0)
    else:
        lax.fori_loop(0, plan.chunks, chunk, 0)
    for copy in copies[5:]:
        copy.wait()


def whole(plan, own, other, row):
    blank = jnp.zeros((plan.ring - plan.cells_a, plan.total_z), jnp.float32)
    return jnp.concatenate([jnp.concatenate([own[row], other[row]], axis=1), blank], axis=0)


def around(plan, center, turn):
    total = pltpu.roll(center, 1, 1) + pltpu.roll(center, plan.total_z - 1, 1)
    return total + turn * (pltpu.roll(center, 1, 0) + pltpu.roll(center, plan.ring - 1, 0))


def start_kernel(plan, pot_own, pot_other, coef, out):
    rad = lax.axis_index("rad")
    rows, weight = plan.cells_r, sweep_weights(SWEEPS)[0]
    plane = functools.partial(whole, plan, pot_own, pot_other)
    for row in range(rows):
        up, down, turn, inverse = (coef[k, pl.ds(plan.guard + row, 1), :] for k in range(4))
        center = plane(row)
        total = around(plan, center, turn)
        if row + 1 < rows:
            total += up * plane(row + 1)
        if row > 0:
            total += down * plane(row - 1)
        out[row] = (1.0 - weight) * center + (weight * inverse) * total
    for side in range(plan.sides):
        place = plan.guard + plan.side_row(side, rad, 1)
        up, down, _, inverse = (coef[k, pl.ds(place, 1), :] for k in range(4))
        factor = jnp.where(plan.sign(side, rad) > 0, down, up)
        out[rows + side] = (weight * inverse * factor) * plane(plan.side_row(side, rad, 0))


def sweeps_kernel(
    plan,
    begun,
    rho_own,
    rho_other,
    coef,
    z_high,
    z_low,
    a_fac,
    r_fac,
    grown,
    force_out,
    first,
    second,
):
    rad = lax.axis_index("rad")
    guard, rows, ring, depth = plan.guard, plan.cells_r, plan.ring, plan.total_z
    weights = sweep_weights(SWEEPS)

    blank = jnp.zeros((ring, depth), jnp.float32)
    for away in range(1, guard + 1):
        for row in (guard - away, guard + rows - 1 + away):
            if away < guard:
                first[row] = blank
            if away != 2:
                second[row] = blank
    for row in range(rows):
        inverse = coef[3, pl.ds(guard + row, 1), :]
        charge = whole(plan, rho_own, rho_other, row)
        first[guard + row] = begun[row] + (weights[0] * inverse) * charge
    for side in range(plan.sides):
        first[guard + plan.side_row(side, rad, 1)] = begun[rows + side]
    for slot in range(plan.slots, grown.shape[0]):
        grown[slot] = blank

    def relaxed(source, row, weight, charge):
        center = source[row]
        up, down, turn, inverse = (coef[k, pl.ds(row, 1), :] for k in range(4))
        total = around(plan, center, turn)
        total += up * source[row + 1] + down * source[row - 1]
        if charge is not None:
            total += charge
        return (1.0 - weight) * center + (weight * inverse) * total

    product = functools.partial(jnp.dot, preferred_element_type=jnp.float32)

    def project(number, group, sums):
        flat = grown[GROUP * group : GROUP * (group + 1)].reshape(GROUP * ring, depth)
        high = flat.astype(jnp.bfloat16)
        low = (flat - high.astype(jnp.float32)).astype(jnp.bfloat16)
        spread = product(high, z_high[number]) + (
            product(high, z_low[number]) + product(low, z_high[number])
        )
        sums = list(sums)
        for slot in range(GROUP * group, min(GROUP * (group + 1), plan.slots)):
            begin = (slot - GROUP * group) * ring
            piece = spread[begin : begin + ring]
            for k, part in enumerate((piece[:, :LANES], piece[:, :LANES], piece[:, LANES:])):
                sums[k] += r_fac[number, k, pl.ds(slot, 1), :] * part
        return sums

    sums = [jnp.zeros((ring, LANES), jnp.float32) for _ in range(3)]
    source, target = first, second
    for sweep in range(1, SWEEPS):
        last = sweep == SWEEPS - 1
        for row in range(rows):
            fresh = relaxed(source, guard + row, weights[sweep], whole(plan, rho_own, rho_other, row))
            if last:
                grown[row] = fresh
                if plan.chunks == 1 and row % GROUP == GROUP - 1:
                    sums = project(0, row // GROUP, sums)
            else:
                target[guard + row] = fresh
        for side in range(plan.sides):
            for step in range(1, sweep + 2):
                place = guard + plan.side_row(side, rad, step)
                fresh = relaxed(source, place, weights[sweep], None)
                if last:
                    slot = SWEEPS * side + step - 1
                    grown[rows + slot] = fresh
                else:
                    target[place] = fresh
        source, target = target, source
    if plan.chunks == 1:
        for group in range(rows // GROUP, plan.planes // GROUP):
            sums = project(0, group, sums)

    def finish(number, sums):
        total = [
            jnp.sum(a_fac[number, turn] * sums[k], axis=0, keepdims=True)
            for k, turn in enumerate((0, 1, 0))
        ]
        total.append(jnp.zeros((5, LANES), jnp.float32))
        force_out[number] = jnp.concatenate(total, axis=0)

    if plan.chunks == 1:
        finish(0, sums)
    else:

        def chunk(number, carry):
            sums = [jnp.zeros((ring, LANES), jnp.float32) for _ in range(3)]
            for group in range(plan.planes // GROUP):
                sums = project(number, group, sums)
            finish(number, sums)
            return carry

        lax.fori_loop(0, plan.chunks, chunk, 0)


def halo_tile(plan, grown, tile, is_even):
    planes = []
    for slot in (2 * tile, 2 * tile + 1):
        half = slice(plan.cells_z, None) if slot < plan.cells_r else slice(plan.cells_z)
        planes.append(grown[slot, plan.cells_a :, half])
    return pack(*planes, is_even)


def join_kernel(plan, grown, force, out):
    is_even = even_sector(lax.axis_index("ang"))
    for tile in range(plan.corners):
        out[tile] = halo_tile(plan, grown, plan.pairs + tile, is_even)[0]
    out[plan.corners :] = force[...]


def main_kernel(plan, grown, after, out):
    is_even = even_sector(lax.axis_index("ang"))
    for tile in range(plan.pairs):
        out[tile] = halo_tile(plan, grown, tile, is_even)[0]


def odd_kernel(plan, grown, after, out):
    is_even = even_sector(lax.axis_index("ang"))
    for tile in range(plan.halo):
        out[tile] = halo_tile(plan, grown, tile, is_even)[1]


def mid_kernel(plan, grown, after, out):
    inner = plan.tiles - 2
    for slot in range(plan.beyond):
        for tile in range(inner):
            first = 8 * (tile + 1)
            out[slot * inner + tile] = grown[plan.cells_r + slot, first : first + 8, plan.cells_z :]


def sum_kernel(plan, even, even_in, out):
    out[...] = even[plan.corners :] + even_in[plan.corners :]


def fold_kernel(plan, grown, even_in, odd_in, *refs):
    forces, edge_out, force_out = refs[:-2], refs[-2], refs[-1]
    is_even = even_sector(lax.axis_index("ang"))
    for slot in range(plan.beyond):
        tile, half = divmod(plan.cells_r + slot, 2)
        first, last = unpack(even_in[tile - plan.pairs], odd_in[tile], half, is_even)
        plane, top = plan.cells_r + slot, plan.cells_a - 8
        edge_out[2 * slot] = grown[plane, :8, plan.cells_z :] + first
        edge_out[2 * slot + 1] = grown[plane, top : plan.cells_a, plan.cells_z :] + last
    force_out[...] = forces[0][...] if len(forces) == 1 else forces[0][...] + forces[1][...]


def meet_kernel(plan, first, second, *refs):
    half = len(refs) // 2
    refs[half][...] = first[...] + second[...]
    for mid, out in zip(refs[:half], refs[half + 1 :]):
        out[...] = mid[...]


def copy_kernel(plan, value, after, out):
    out[...] = value[...]


def final_kernel(plan, *refs):
    own, mids, edges = refs[0], refs[1 : 1 + plan.sides], refs[1 + plan.sides : 1 + 2 * plan.sides]
    even_in, odd_in, force, out, force_out = refs[-5:]
    force_out[...] = force[...]
    rad = lax.axis_index("rad")
    is_even = even_sector(lax.axis_index("ang"))
    top, inner = plan.cells_a - 8, plan.tiles - 2
    for row in range(plan.cells_r):
        first, last = unpack(even_in[row // 2], odd_in[row // 2], row % 2, is_even)
        out[row] = own[row, : plan.cells_a, : plan.cells_z]
        out[row, 0:8, :] += first
        out[row, top:, :] += last
    for side in range(plan.sides):
        for step in range(1, SWEEPS + 1):
            row = plan.landing_row(side, rad, step)
            out[row, 0:8, :] += edges[side][2 * step - 2]
            out[row, top:, :] += edges[side][2 * step - 1]
            for tile in range(inner):
                out[row, 8 * tile + 8 : 8 * tile + 16, :] += mids[side][(step - 1) * inner + tile]


def share_kernel(plan, force, part, out):
    share = out.shape[1]
    start = plan.device(*(lax.axis_index(name) for name in AXES)) * share
    total = force[start // LANES] + part[start // LANES]
    turned = pltpu.roll(total, lax.rem(LANES - lax.rem(start, LANES), LANES), 1)
    out[...] = turned[:3, :share]


def call(kernel, plan, outs, scratch, flops, bytes_moved, args, spaces=None, megabytes=24):
    in_vmem = pl.BlockSpec(memory_space=pltpu.VMEM)
    return pl.pallas_call(
        functools.partial(kernel, plan),
        out_shape=[
            out if hasattr(out, "dtype") else jax.ShapeDtypeStruct(out, jnp.float32) for out in outs
        ],
        in_specs=spaces or [in_vmem] * len(args),
        out_specs=[in_vmem] * len(outs),
        scratch_shapes=scratch,
        compiler_params=pltpu.CompilerParams(vmem_limit_bytes=megabytes * 2**20),
        cost_estimate=pl.CostEstimate(flops=flops, bytes_accessed=bytes_moved, transcendentals=0),
    )(*args)


def shards(plan, potential, density, anchor, extent, center, charge, place):
    ring, depth, slots, chunks = plan.ring, plan.total_z, plan.slots, plan.chunks
    rows, width, block = plan.cells_r, plan.cells_z, potential.shape
    swap = [(0, 1), (1, 0)]
    potential_other = lax.ppermute(potential, "ax", swap)
    density_other = lax.ppermute(density, "ax", swap)
    tables = (anchor, extent, center, charge.reshape(1, -1), place.reshape(1, -1))
    tall = rows + 2 * plan.guard
    axial = jax.ShapeDtypeStruct((chunks, depth, 2 * LANES), jnp.bfloat16)
    *factors, coef, potential, density = call(
        factors_kernel,
        plan,
        [axial, axial, (chunks, 2, ring, LANES), (chunks, 3, slots, LANES)]
        + [(4, tall, depth), block, block],
        [pltpu.VMEM(table.shape, table.dtype) for table in tables] + [pltpu.SemaphoreType.DMA((7,))],
        10**6,
        10**6,
        [pltpu.with_memory_space_constraint(value, pltpu.HBM) for value in (*tables, potential, density)],
        [pl.BlockSpec(memory_space=pl.ANY)] * 7,
    )
    (begun,) = call(
        start_kernel,
        plan,
        [(rows + plan.sides, ring, depth)],
        [],
        10**7,
        10**7,
        (potential, potential_other, coef),
    )
    scratch = [(tall, ring, depth)] * 2
    inner = SWEEPS * (plan.tiles - 2)
    grown, force = call(
        sweeps_kernel,
        plan,
        [(plan.planes, ring, depth), (chunks, 8, LANES)],
        [pltpu.VMEM(shape, jnp.float32) for shape in scratch],
        10**9,
        10**7,
        (begun, density, density_other, coef, *factors),
    )

    def send(value, move):
        return lax.ppermute(value, AXES, plan.moves(move))

    def send_radial(value, length):
        if plan.sides == 0:
            return []
        if plan.sides == 1:
            return [send(value, lambda r, a: (1 - r, a))]
        last = plan.n_rad - 1
        return [
            send(value[length : 2 * length], lambda r, a: (r - 1, a) if r else None),
            send(value[:length], lambda r, a: (r + 1, a) if r < last else None),
        ]

    def send_angular(value, step):
        return send(value, lambda r, a: (r, a ^ step))

    (join,) = call(
        join_kernel, plan, [(plan.corners + chunks, 8, width)], [], 10**5, 10**5, (grown, force)
    )
    join_in = send_angular(join, 1)
    odd_shape = (plan.halo, 8, width)
    (odd,) = call(odd_kernel, plan, [odd_shape], [], 10**6, 10**6, (grown, join))
    odd_in = send(odd, lambda r, a: (r, (a + 1 - 2 * (1 - a % 2)) % plan.n_ang))
    (force,) = call(sum_kernel, plan, [force.shape], [], 10**9, 10**9, (join, join_in))
    mid_shape = (max(1, inner * plan.sides), 8, width)
    (mid,) = call(mid_kernel, plan, [mid_shape], [], 10**6, 10**6, (grown, force))
    (even,) = call(
        main_kernel, plan, [(plan.pairs, 8, width)], [], 10**6, 10**6, (grown, force)
    )
    mids = send_radial(mid, inner) + [send_angular(even, 1)]
    parts = [force]
    step = plan.n_ang // 2
    while step > 2:
        force = sum(parts)
        parts = [force, send_angular(force, step)]
        step //= 2
    (odd_in,) = call(copy_kernel, plan, [odd.shape], [], 10**9, 10**9, (odd_in, odd))
    edge, force = call(
        fold_kernel,
        plan,
        [(max(1, 2 * plan.beyond), 8, width), (chunks, 8, LANES)],
        [],
        10**5,
        10**5,
        (grown, join_in, odd_in, *parts),
    )
    (edge,) = call(copy_kernel, plan, [edge.shape], [], 10**6, 10**6, (edge, force))
    edges = send_radial(edge, 2 * SWEEPS)
    step = 1
    while step < plan.n_rad:
        part = send(force, lambda r, a: (r ^ step, a))
        step *= 2
        if step < plan.n_rad:
            force = force + part
        else:
            shapes = [value.shape for value in (force, *mids)]
            force, *mids = call(meet_kernel, plan, shapes, [], 10**9, 10**9, (force, part, *mids))
    *mids, even_in = mids
    last_part = send_angular(force, 2) if plan.n_ang > 2 else jnp.zeros_like(force)
    final, force = call(
        final_kernel,
        plan,
        [block, force.shape],
        [],
        10**5,
        10**6,
        (grown, *mids, *edges, even_in, odd_in, force),
    )
    share = plan.atoms // (plan.n_rad * plan.n_ang * plan.n_ax)
    (mine,) = call(share_kernel, plan, [(3, share)], [], 10**5, 10**5, (force, last_part))
    return final, mine


def solution(mesh):
    whole = P("rad", "ang", "ax")

    def run(potential, density, anchor, extent, center, charge, place):
        sizes = [mesh.shape[name] for name in AXES]
        block = [total // parts for total, parts in zip(potential.shape, sizes)]
        plan = Plan(mesh, block, charge.shape[0])
        return jax.shard_map(
            functools.partial(shards, plan),
            mesh=mesh,
            in_specs=(whole, whole, P(), P(), P(), P(), P()),
            out_specs=(whole, P(None, AXES)),
            check_vma=False,
        )(potential, density, anchor, extent, center, charge, place)

    return run
```
